128 devices in a mesh: seq: 16 (over x, y), section: 8 (over z, core).
Axes of the slice: x: 4, y: 4, z: 4, core: 2. Of those that a mesh axis runs over, the one named last changes fastest.
Arguments:
- hidden: bfloat16 [8, 6144, 2560], P('section', 'seq'), may hold values from -6 to 6
- query_norm_gain: float32 [8, 2560], P('section'), may hold values from 0.25 to 1.75
- key_norm_gain: float32 [8, 2560], P('section'), may hold values from 0.25 to 1.75
- text_kv: bfloat16 [8, 16, 2, 512, 2560], P('section', 'seq'), may hold values from -6 to 6
- holder: int32 [8], P('section'), may hold values from 0 to 15
- pattern: int32 [48, 7], replicated, may hold values from 0 to 1, as said below
- grad_out: bfloat16 [8, 6144, 2560], P('section', 'seq'), may hold values from -6 to 6
Outputs:
- attended: bfloat16 [8, 6144, 2560], P('section', 'seq')
- upstream: bfloat16 [8, 6144, 2560], P('section', 'seq')
- text_grad: bfloat16 [8, 2, 512, 2560], P('section')
The draws below stay inside these ranges and needn't reach their ends.
Inputs may be any that keep to these rules, and one draw needn't show every extreme that they name: pattern[b, 3] = 1 for every block b; entries are 0 or 1.
All inputs are finite; a program needn't handle non-finite values.
Results may differ from the reference program's by a relative error of at most 0.0078.
Values may be sent and summed in bfloat16 or wider, within the bound.
A program may use at most 256 MiB of HBM per device.

```python
import jax
import jax.numpy as jnp
from jax import lax

HDIM = 128
BLK = 128
TXT = 512
T_DEV = 384
HD = 2560
BPD = 3
TOKENS = 6144
NQB = 48
N_SEQ = 16
N_SECTION = 8


def draw_pattern(key, part):
    first, second = jax.random.split(jax.random.fold_in(key, 17))
    slabs = NQB // BPD
    rate = jax.random.randint(first, (slabs, 1, 1), 20, 96)
    values = jax.random.randint(second, (slabs, BPD, 2 * BPD + 1), 0, 100)
    picked = (values < rate).astype(jnp.int32)
    picked = picked.at[:, :, BPD].set(1)
    return picked.reshape(NQB, 2 * BPD + 1)


def draw_hidden(key, part):
    own_rows = jax.random.fold_in(key, 11)
    shape = (N_SECTION, TOKENS, HD)
    values = jax.random.truncated_normal(own_rows, -6.0, 6.0, shape, jnp.float32)
    return values.astype(jnp.bfloat16)


def draw_text_kv(key, part):
    own_rows = jax.random.fold_in(key, 23)
    shape = (N_SECTION, N_SEQ, 2, TXT, HD)
    values = jax.random.truncated_normal(own_rows, -6.0, 6.0, shape, jnp.float32)
    return values.astype(jnp.bfloat16)


def set_ends(entries, stream_key, smallest, largest):
    longest = entries.shape.index(max(entries.shape))
    spots = []
    for shift in (0, 1):
        where = [jax.random.randint(jax.random.fold_in(stream_key, axis), (), 0, length) for axis, length in enumerate(entries.shape)]
        where[longest] = (where[longest] + shift) % entries.shape[longest]
        spots.append(tuple(where))
    return entries.at[spots[0]].set(smallest).at[spots[1]].set(largest)


def steps_of(key, dims, cuts, least, largest):
    loudness = 1.0
    for axis_at, blocks in cuts:
        steps = jax.random.uniform(jax.random.fold_in(jax.random.fold_in(key, 6), axis_at), (blocks,), jnp.float32, least / len(cuts), largest / len(cuts))
        loudness = loudness * jnp.repeat(jnp.exp(steps), dims[axis_at] // blocks).reshape((-1,) + (1,) * (len(dims) - 1 - axis_at))
    return loudness


def scatter_about(rng, shape, scale, bound, cuts=(), kind=jnp.bfloat16):
    entries = jax.random.normal(rng, shape, jnp.float32) * scale
    if len(cuts) > 0:
        entries = steps_of(rng, shape, cuts, -0.22, 0.18) * entries
    return jnp.clip(entries, min=-bound, max=bound).astype(kind)


def setup_inputs(seed: int = 0) -> dict:
    seeds = jax.random.split(jax.random.key(seed), 8)
    return {
        "hidden": draw_hidden(jax.random.fold_in(seeds[7], 71), 0),
        "query_norm_gain": jnp.clip(1.0 + 0.15 * jax.random.normal(seeds[1], (N_SECTION, HD), jnp.float32), 0.25, 1.75),
        "key_norm_gain": jnp.clip(1.0 + 0.15 * jax.random.normal(seeds[2], (N_SECTION, HD), jnp.float32), 0.25, 1.75),
        "text_kv": draw_text_kv(jax.random.fold_in(seeds[7], 71), 0),
        "holder": set_ends(jax.random.randint(seeds[4], (N_SECTION,), 0, N_SEQ), jax.random.fold_in(seeds[4], 1), 0, N_SEQ - 1).astype(jnp.int32),
        "pattern": draw_pattern(jax.random.fold_in(seeds[7], 71), 0),
        "grad_out": scatter_about(seeds[6], (N_SECTION, TOKENS, HD), 1.0, 6.0, ((0, 8), (1, 16))),
    }


eps = 1e-06

def norm_forward(hidden_state, norm_gain):
    hidden_float = hidden_state.astype(jnp.float32)
    inverse_root_norm = lax.rsqrt(lax.optimization_barrier(jnp.mean(hidden_float * hidden_float, axis=-1, keepdims=True)) + eps)
    normalized_input = hidden_float * inverse_root_norm
    return ((normalized_input * norm_gain).astype(jnp.bfloat16), normalized_input, inverse_root_norm)

def norm_backward(upper_bound, norm_gain, normalized_input, inverse_root_norm):
    scaled_input = upper_bound * norm_gain
    return inverse_root_norm * (scaled_input - normalized_input * lax.optimization_barrier(jnp.mean(scaled_input * normalized_input, axis=-1, keepdims=True)))

def block_mask(pattern, slab, bpd, nslab):
    span = pattern.shape[1]
    rows = lax.dynamic_slice_in_dim(pattern, (slab * bpd).astype(jnp.int32), bpd, 0)
    first = jnp.arange(bpd, dtype=jnp.int32)[:, None]
    second = jnp.arange(3 * bpd, dtype=jnp.int32)[None, :]
    offset = second - first
    onehot = offset[:, :, None] == jnp.arange(span, dtype=jnp.int32)[None, None, :]
    picked = lax.optimization_barrier(jnp.sum(jnp.where(onehot, rows[:, None, :], 0), axis=-1))
    globe = slab * bpd - bpd + second
    inside = (globe >= 0) & (globe < nslab * bpd)
    return (picked > 0) & inside

def token_mask(blocks):
    return jnp.repeat(jnp.repeat(blocks, BLK, axis=0), BLK, axis=1)

def divide_heads(x):
    return x.reshape(x.shape[0], x.shape[1] // HDIM, HDIM).transpose(1, 0, 2)

def join_heads(x):
    return x.transpose(1, 0, 2).reshape(x.shape[1], x.shape[0] * x.shape[2])

def query_side(qh, kh, vh, tkh, tvh, doh, attend_mask):
    scale = qh.shape[-1] ** (-0.5)
    keys = jnp.concatenate([kh, tkh], axis=0)
    vals = jnp.concatenate([vh, tvh], axis=0)
    full = jnp.concatenate([attend_mask, jnp.ones((qh.shape[0], tkh.shape[0]), bool)], axis=1)
    scores = jnp.dot(qh, keys.T, preferred_element_type=jnp.float32) * scale
    scores = jnp.where(full, scores, -1e+30)
    top = lax.optimization_barrier(jnp.max(scores, axis=1, keepdims=True))
    total = lax.optimization_barrier(jnp.sum(jnp.where(full, jnp.exp(scores - top), 0.0), axis=1, keepdims=True))
    lse = top + jnp.log(total)
    probs = jnp.where(full, jnp.exp(scores - lse), 0.0)
    probs_b = probs.astype(jnp.bfloat16)
    out = jnp.dot(probs_b, vals, preferred_element_type=jnp.float32)
    dprob = jnp.dot(doh, vals.T, preferred_element_type=jnp.float32)
    delta = lax.optimization_barrier(jnp.sum(doh.astype(jnp.float32) * out, axis=1))
    dscore = (probs * (dprob - delta[:, None]) * scale).astype(jnp.bfloat16)
    query_gradient = jnp.dot(dscore, keys, preferred_element_type=jnp.float32)
    dkeys = jnp.dot(dscore.T, qh, preferred_element_type=jnp.float32)
    dvals = jnp.dot(probs_b.T, doh, preferred_element_type=jnp.float32)
    return (out, lse[:, 0], delta, query_gradient, dkeys, dvals)

def slab_backward(normed_query, extended_keys, extended_values, text_tokens, output_gradient, attend_mask):

    def each_head_value(a):
        return query_side(a[0], a[1], a[2], a[3], a[4], a[5], attend_mask)
    saved_residuals = lax.map(each_head_value, (divide_heads(normed_query), divide_heads(extended_keys), divide_heads(extended_values), divide_heads(text_tokens[0]), divide_heads(text_tokens[1]), divide_heads(output_gradient)))
    out, lse, delta, query_gradient, dkeys, dvals = saved_residuals
    ext_rows = extended_keys.shape[0]
    ext = jnp.stack([join_heads(dkeys[:, :ext_rows]), join_heads(dvals[:, :ext_rows])])
    dtext = jnp.stack([join_heads(dkeys[:, ext_rows:]), join_heads(dvals[:, ext_rows:])])
    return (join_heads(out), join_heads(query_gradient), ext, dtext)

def reference(hidden, query_norm_gain, key_norm_gain, text_kv, holder, pattern, grad_out):
    token_rows = T_DEV
    width = hidden.shape[2]
    outs = []
    grads = []
    texts_out = []
    for section_index in range(N_SECTION):
        hidden_state = hidden[section_index]
        output_gradient = grad_out[section_index]
        normed_query, normalized_input, inverse_root_norm = norm_forward(hidden_state, query_norm_gain[section_index])
        kn, _, _ = norm_forward(hidden_state, key_norm_gain[section_index])
        text_tokens = lax.dynamic_index_in_dim(text_kv[section_index], holder[section_index], 0, keepdims=False)
        zero_block = jnp.zeros((token_rows, width), jnp.bfloat16)
        kpad = jnp.concatenate([zero_block, kn, zero_block], axis=0)
        padded_values = jnp.concatenate([zero_block, hidden_state, zero_block], axis=0)

        def one(slab):
            start_row = (slab * token_rows).astype(jnp.int32)
            scaled_query = lax.dynamic_slice_in_dim(normed_query, start_row, token_rows, 0)
            score_gradient = lax.dynamic_slice_in_dim(output_gradient, start_row, token_rows, 0)
            extended_keys = lax.dynamic_slice_in_dim(kpad, start_row, 3 * token_rows, 0)
            extended_values = lax.dynamic_slice_in_dim(padded_values, start_row, 3 * token_rows, 0)
            attend_mask = token_mask(block_mask(pattern, slab, BPD, N_SEQ))
            return slab_backward(scaled_query, extended_keys, extended_values, text_tokens, score_gradient, attend_mask)
        out, query_gradient, ext, dtext = lax.map(one, jnp.arange(N_SEQ, dtype=jnp.int32))
        edge = jnp.zeros((1, 2, token_rows, width), jnp.float32)
        own_rows = ext[:, :, token_rows:2 * token_rows]
        own_rows = own_rows + jnp.concatenate([ext[1:, :, :token_rows], edge], axis=0)
        own_rows = own_rows + jnp.concatenate([edge, ext[:-1, :, 2 * token_rows:]], axis=0)
        normed_key_gradient = own_rows[:, 0].reshape(N_SEQ * token_rows, width)
        value_gradient = own_rows[:, 1].reshape(N_SEQ * token_rows, width)
        query_gradient = query_gradient.reshape(N_SEQ * token_rows, width)
        head_dimension = value_gradient + norm_backward(query_gradient, query_norm_gain[section_index], normalized_input, inverse_root_norm) + norm_backward(normed_key_gradient, key_norm_gain[section_index], normalized_input, inverse_root_norm)
        outs.append(out.reshape(N_SEQ * token_rows, width).astype(jnp.bfloat16))
        grads.append(head_dimension.astype(jnp.bfloat16))
        texts_out.append(lax.optimization_barrier(jnp.sum(dtext, axis=0)).astype(jnp.bfloat16))
    ups = [grads[s + 1] for s in range(N_SECTION - 1)] + [jnp.zeros_like(grads[0])]
    return (jnp.stack(outs), jnp.stack(ups), jnp.stack(texts_out))
```

```python
import jax
import jax.numpy as jnp
from jax import lax
from jax.experimental import pallas as pl
from jax.experimental.pallas import tpu as pltpu
from jax.sharding import PartitionSpec as P

HDIM = 128
BLK = 128
EPS = 1e-06
MESH = pl.DeviceIdType.MESH

NX = 4
NY = 4
SLAB = 384
TXT = 512
WIDTH = 2560
STEPS = 5
OWN = NY * SLAB
EXT = OWN + 2 * SLAB
KEYS = EXT + TXT
QT = 256
KC = 256
NCHUNK = 4 + TXT // KC
SCALE = HDIM ** (-0.5)
LOG2E = 1.4426950408889634
NEG = -1e30

(
    K_H,
    K_DO,
    K_TX,
    K_TY,
    K_TG,
    K_HALO,
    K_ATT,
    K_AH,
    K_A,
    K_RS,
    K_G1,
    K_G2,
) = range(12)
KINDS = 12
O_R, O_RH, O_MH, O_M = range(4)

f32 = jnp.float32
bf16 = jnp.bfloat16


def dot_nn(a, b):
    return lax.dot_general(a, b, (((1,), (0,)), ((), ())), preferred_element_type=f32)


def dot_nt(a, b):
    return lax.dot_general(a, b, (((1,), (1,)), ((), ())), preferred_element_type=f32)


def block(k):
    return pl.ds(pl.multiple_of(k * BLK, BLK), BLK)


def span(start, size, unit):
    return pl.ds(pl.multiple_of(start, unit), size)


def packed(column):
    rows = column.shape[0]
    wide = jnp.broadcast_to(column, (rows, BLK))
    return [wide[b * BLK : (b + 1) * BLK].T[:8] for b in range(rows // BLK)]


def unpacked(tile):
    return jnp.broadcast_to(tile[:1], (BLK, BLK)).T


def kernel(
    hid, do_in, txt, gq_ref, gk_ref, sel_ref, qb_ref,
    att_out, dh_out, tg_out,
    HS, HX, DO, RTX, RT, RB, T1, TS, T2, T3, KA, KT, VT, QA, S, PB, DK, DV, DQ,
    ATT, AFS, AH, AHR, AO, AF, M, MH, MT, MHS, MHR, MR, TGP, TG1, TG2, TGY, TGX, DH,
    send, recv, once_send, once_recv, loc, loc1,
):
    seq = lax.axis_index("seq")
    x = lax.div(seq, NY)
    y = lax.rem(seq, NY)

    def ry(d):
        return lax.rem(y + (d + NY), NY)

    def rx(d):
        return lax.rem(x + (d + NX), NX)

    def yid(d):
        return {"seq": x * NY + ry(d)}

    def xid(d):
        return {"seq": rx(d) * NY + y}

    def rc(src, dst, kind, j, d, dev):
        return pltpu.make_async_remote_copy(
            src_ref=src, dst_ref=dst, send_sem=send.at[kind, j, d],
            recv_sem=recv.at[kind, j, d], device_id=dev, device_id_type=MESH,
        )

    def rc1(src, dst, kind, d, dev):
        return pltpu.make_async_remote_copy(
            src_ref=src, dst_ref=dst, send_sem=once_send.at[kind, d],
            recv_sem=once_recv.at[kind, d], device_id=dev, device_id_type=MESH,
        )

    def hcol(j, yy):
        return block(NY * j + yy)

    def wide(j):
        return span(j * (NY * BLK), NY * BLK, NY * BLK)

    def slab(yy):
        return span(SLAB + SLAB * yy, SLAB, SLAB)

    def oslab(yy):
        return span(SLAB * yy, SLAB, SLAB)

    def cp_h(j, d, w=False):
        return rc(hid.at[:, hcol(j, ry(d))], HX.at[j, slab(ry(-d) if w else y), :], K_H, j, d, yid(d))

    def cp_do(j, d, w=False):
        return rc(do_in.at[:, hcol(j, ry(d))], DO.at[j, oslab(ry(-d) if w else y), :], K_DO, j, d, yid(d))

    def cp_tx(j, d, w=False):
        return rc(txt.at[:, block(rx(d)), wide(j)], T1.at[j, rx(-d) if w else x], K_TX, j, d, xid(d))

    def cp_ty(j, d, w=False):
        return rc(TS.at[j, :, :, block(ry(d))], T2.at[j, ry(-d) if w else y], K_TY, j, d, yid(d))

    def cp_tg(j, d, w=False):
        return rc(T3.at[j, :, block(x), :], T3.at[j, :, block(rx(-d) if w else x), :], K_TG, j, d, xid(d))

    def cp_halo(j, d, w=False):
        if d == 1:
            return rc(HX.at[j, pl.ds(OWN, SLAB), :], HX.at[j, pl.ds(0, SLAB), :], K_HALO, j, 1, xid(1))
        return rc(HX.at[j, pl.ds(SLAB, SLAB), :], HX.at[j, pl.ds(OWN + SLAB, SLAB), :], K_HALO, j, 3, xid(3))

    def cp_att(j, d, w=False):
        return rc(ATT.at[j, oslab(ry(d)), :], att_out.at[:, hcol(j, ry(-d) if w else y)], K_ATT, j, d, yid(d))

    def cp_ah(j, d, w=False):
        k = 1 if d == 1 else 0
        return rc(AH.at[j, k], AHR.at[j, 1 - k], K_AH, j, d, xid(d))

    def cp_a(j, d, w=False):
        return rc(AO.at[j, oslab(ry(d)), :], AF.at[:, hcol(j, ry(-d) if w else y)], K_A, j, d, yid(d))

    def cp_rs(j, d, w=False):
        return rc(TGP.at[j, :, block(rx(d)), :], TG1.at[j, rx(-d) if w else x], K_RS, j, d, xid(d))

    def cp_g1k(j, d, w=False):
        return rc(TG2.at[j, 0], TGY.at[j, :, block(ry(-d) if w else y)], K_G1, j, d, yid(d))

    def cp_g1v(j, d, w=False):
        return rc(TG2.at[j, 1], TGX.at[j, block(rx(-d) if w else x), :], K_G1, j, 4 + d, xid(d))

    def cp_g2k(j, d, w=False):
        return rc(TGY.at[j], tg_out.at[0, block(rx(-d) if w else x), wide(j)], K_G2, j, d, xid(d))

    def cp_g2v(j, d, w=False):
        return rc(TGX.at[j], tg_out.at[1, :, hcol(j, ry(-d) if w else y)], K_G2, j, 4 + d, yid(d))

    def cp_r(d, w=False):
        return rc1(RT, RTX.at[span(24 + 24 * (ry(-d) if w else y), 24, 8), :], O_R, d, yid(d))

    def cp_rh(d, w=False):
        if d == 1:
            return rc1(RTX.at[pl.ds(96, 24), :], RTX.at[pl.ds(0, 24), :], O_RH, 1, xid(1))
        return rc1(RTX.at[pl.ds(24, 24), :], RTX.at[pl.ds(120, 24), :], O_RH, 3, xid(3))

    def cp_mh(d, w=False):
        k = 1 if d == 1 else 0
        return rc1(MHS.at[k], MHR.at[1 - k], O_MH, d, xid(d))

    def cp_m(d, w=False):
        return rc1(MT.at[span(24 * ry(d), 24, 8), :], MR.at[ry(-d) if w else y], O_M, d, yid(d))

    def lo_h(j):
        return pltpu.make_async_copy(hid.at[:, hcol(j, y)], HX.at[j, slab(y), :], loc.at[0, j])

    def lo_do(j):
        return pltpu.make_async_copy(do_in.at[:, hcol(j, y)], DO.at[j, oslab(y), :], loc.at[1, j])

    def lo_tx(j):
        return pltpu.make_async_copy(txt.at[:, block(x), wide(j)], T1.at[j, x], loc.at[2, j])

    def lo_att(j):
        return pltpu.make_async_copy(ATT.at[j, oslab(y), :], att_out.at[:, hcol(j, y)], loc.at[3, j])

    def lo_g2k(j):
        return pltpu.make_async_copy(TGY.at[j], tg_out.at[0, block(x), wide(j)], loc.at[4, j])

    def lo_g2v(j):
        return pltpu.make_async_copy(TGX.at[j], tg_out.at[1, :, hcol(j, y)], loc.at[5, j])

    ALL = (1, 3, 2)
    SIDES = (1, 3)

    def stage_a(j):
        lo_tx(j).wait()
        for d in ALL:
            cp_tx(j, d, True).wait_recv()
        for kv in range(2):
            part = jnp.zeros((BLK, NY * BLK), f32)
            for k in range(NX):
                part = part + T1[j, k, kv].astype(f32) * sel_ref[k : k + 1, :]
            TS[j, kv] = part.astype(bf16)
        T2[j, y] = TS[j, :, :, block(y)]
        for d in ALL:
            cp_ty(j, d).start()
        lo_h(j).wait()
        for d in ALL:
            cp_h(j, d, True).wait_recv()
        for d in SIDES:
            cp_halo(j, d).start()

    def stage_b(j):
        for d in ALL:
            cp_ty(j, d, True).wait_recv()
        for kv in range(2):
            part = jnp.zeros((BLK, BLK), f32)
            for k in range(NY):
                part = part + T2[j, k, kv].astype(f32) * sel_ref[NX + k : NX + k + 1, :BLK]
            T3[j, kv, block(x), :] = part.astype(bf16)
        for d in ALL:
            cp_tg(j, d).start()

    def stage_c(j):
        for d in SIDES:
            cp_halo(j, d, True).wait_recv()
        lo_do(j).wait()
        for d in ALL:
            cp_do(j, d, True).wait_recv()
            cp_tg(j, d, True).wait_recv()
        head = NY * j + y
        gq = gq_ref[pl.ds(head, 1), :]
        gk = gk_ref[pl.ds(head, 1), :]
        par = lax.rem(j, 2)

        def prep(b, _):
            rows = block(b)
            h = HX[j, rows, :].astype(f32)
            kn = (h * RB[rows, :]) * gk
            KA[rows, :BLK] = kn.astype(bf16)
            KT[:, rows] = kn.T.astype(bf16)
            VT[:BLK, rows] = h.T.astype(bf16)
            return 0

        lax.fori_loop(0, EXT // BLK, prep, 0)
        for b in range(TXT // BLK):
            rows = slice(EXT + b * BLK, EXT + (b + 1) * BLK)
            kn = T3[j, 0, b * BLK : (b + 1) * BLK, :]
            KA[rows, :BLK] = kn
            KT[:, rows] = kn.astype(f32).T.astype(bf16)
            VT[:BLK, rows] = T3[j, 1, b * BLK : (b + 1) * BLK, :].astype(f32).T.astype(bf16)

        def clear(b, _):
            rows = span(b * KC, KC, KC)
            DK[rows, :] = jnp.zeros((KC, BLK), f32)
            DV[rows, :] = jnp.zeros((KC, BLK), f32)
            return 0

        lax.fori_loop(0, KEYS // KC, clear, 0)

        def tile(u, _):
            q0 = u * QT
            qrows = span(q0, QT, QT)
            erows = span(SLAB + q0, QT, BLK)
            h = HX[j, erows, :].astype(f32)
            qn = ((h * RB[erows, :]) * gq).astype(bf16)
            QA[:, :BLK] = qn
            QA[:, BLK:] = qb_ref[qrows, :]
            qa = QA[...]
            chunks = [span(q0 + KC * c, KC, KC) for c in range(4)]
            chunks += [pl.ds(EXT + KC * c, KC) for c in range(TXT // KC)]
            top = None
            for c in range(NCHUNK):
                s = dot_nt(KA[chunks[c], :], qa)
                S[c] = s
                high = jnp.max(s, axis=0, keepdims=True)
                top = high if top is None else jnp.maximum(top, high)
            top = top * (SCALE * LOG2E)
            ot = None
            for c in range(NCHUNK):
                p = jnp.exp2(S[c] * (SCALE * LOG2E) - top).astype(bf16)
                PB[c] = p
                term = dot_nn(VT[:, chunks[c]], p)
                ot = term if ot is None else ot + term
            inv = 1.0 / ot[BLK : BLK + 1, :]
            o = ot[:BLK, :] * inv
            dt = DO[j, qrows, :].astype(f32).T
            delta = jnp.sum(dt * o, axis=0, keepdims=True) * inv
            dts = (dt * inv).astype(bf16)
            ATT[j, qrows, :] = o.T.astype(bf16)
            dq = None
            for c in range(NCHUNK):
                if c < 4:
                    v = HX[j, chunks[c], :]
                else:
                    v = T3[j, 1, (c - 4) * KC : (c - 3) * KC, :]
                p = PB[c]
                dp = dot_nn(v, dts)
                ds = (p.astype(f32) * (dp - delta)).astype(bf16)
                DV[chunks[c], :] += dot_nt(p, dts)
                DK[chunks[c], :] += dot_nn(ds, qn)
                term = dot_nn(KT[:, chunks[c]], ds)
                dq = term if dq is None else dq + term
            DQ[qrows, :] = dq.T
            return 0

        lax.fori_loop(0, OWN // QT, tile, 0)

        for d in ALL:
            cp_att(j, d).start()
        lo_att(j).start()

        for k in range(2):
            rows = slice(k * (OWN + SLAB), k * (OWN + SLAB) + SLAB)
            r = RB[rows, :]
            t = (gk * DK[rows, :]) * SCALE
            AH[j, k] = (DV[rows, :] + r * t).astype(bf16)
            MH[k] += (HX[j, rows, :].astype(f32) * r) * t
        for d in SIDES:
            cp_ah(j, d).start()
        TGP[j, 0] = (DK[EXT:, :] * SCALE).astype(bf16)
        TGP[j, 1] = DV[EXT:, :].astype(bf16)
        TG1[j, x] = TGP[j, :, block(x), :]
        for d in ALL:
            cp_rs(j, d).start()

        def own(i, _):
            rows = slab(i)
            qrows = oslab(i)
            r = RB[rows, :]
            t = (gq * DQ[qrows, :] + gk * DK[rows, :]) * SCALE
            AFS[par, qrows, :] = DV[rows, :] + r * t
            M[qrows, :] += (HX[j, rows, :].astype(f32) * r) * t
            return 0

        lax.fori_loop(0, NY, own, 0)

    def stage_d(j):
        par = lax.rem(j, 2)
        for d in SIDES:
            cp_ah(j, d, True).wait_recv()
        for i in range(NY):
            rows = slice(i * SLAB, (i + 1) * SLAB)
            a = AFS[par, rows, :]
            if i == 0:
                a = a + AHR[j, 0].astype(f32)
            if i == NY - 1:
                a = a + AHR[j, 1].astype(f32)
            AO[j, rows, :] = a.astype(bf16)
        for d in ALL:
            cp_a(j, d).start()
        AF[:, hcol(j, y)] = AO[j, oslab(y), :]
        for d in ALL:
            cp_rs(j, d, True).wait_recv()
        for kv in range(2):
            total = TG1[j, 0, kv].astype(f32)
            for k in range(1, NX):
                total = total + TG1[j, k, kv].astype(f32)
            TG2[j, kv] = total.astype(bf16)
        TGY[j, :, block(y)] = TG2[j, 0]
        TGX[j, block(x), :] = TG2[j, 1]
        for d in ALL:
            cp_g1k(j, d).start()
            cp_g1v(j, d).start()

    def stage_e(j):
        for d in ALL:
            cp_g1k(j, d, True).wait_recv()
            cp_g1v(j, d, True).wait_recv()
        for d in ALL:
            cp_g2k(j, d).start()
            cp_g2v(j, d).start()
        lo_g2k(j).start()
        lo_g2v(j).start()

    barrier = pltpu.get_barrier_semaphore()
    for d in ALL:
        pl.semaphore_signal(barrier, inc=1, device_id=yid(d), device_id_type=MESH)
        pl.semaphore_signal(barrier, inc=1, device_id=xid(d), device_id_type=MESH)
    load = pltpu.make_async_copy(hid, HS, loc1.at[0])
    load.start()

    def first_local(j, _):
        lo_h(j).start()
        lo_tx(j).start()
        lo_do(j).start()
        return 0

    lax.fori_loop(0, STEPS, first_local, 0)
    pl.semaphore_wait(barrier, 6)

    def first(j, _):
        for d in ALL:
            cp_tx(j, d).start()
            cp_h(j, d).start()
        for d in ALL:
            cp_do(j, d).start()
        return 0

    lax.fori_loop(0, STEPS, first, 0)

    lane = lax.broadcasted_iota(jnp.int32, (BLK, BLK), 1)

    def marks(b, _):
        KA[block(b), BLK:] = jnp.where(lane == b, 1.0, 0.0).astype(bf16)
        return 0

    lax.fori_loop(0, EXT // BLK, marks, 0)
    KA[EXT:, BLK:] = jnp.zeros((TXT, BLK), bf16)
    VT[BLK:, :] = jnp.ones((16, KEYS), bf16)

    def clear_m(i, _):
        M[oslab(i), :] = jnp.zeros((SLAB, BLK), f32)
        return 0

    lax.fori_loop(0, NY, clear_m, 0)
    for k in range(2):
        MH[k] = jnp.zeros((SLAB, BLK), f32)

    load.wait()

    for b in range(SLAB // BLK):
        h = HS[b * BLK : (b + 1) * BLK, :].astype(f32)
        mean = jnp.sum(h * h, axis=1, keepdims=True) * (1.0 / WIDTH)
        RT[8 * b : 8 * b + 8, :] = packed(lax.rsqrt(mean + EPS))[0]
    for d in ALL:
        cp_r(d).start()
    RTX[span(24 + 24 * y, 24, 8), :] = RT[...]
    for d in ALL:
        cp_r(d, True).wait_recv()
    for d in SIDES:
        cp_rh(d).start()
    for d in SIDES:
        cp_rh(d, True).wait_recv()
    for b in range(EXT // BLK):
        RB[b * BLK : (b + 1) * BLK, :] = unpacked(RTX[8 * b : 8 * b + 8, :])

    stage_a(0)
    stage_b(0)
    stage_a(1)

    def step(j, _):
        stage_c(j)

        @pl.when(j + 1 < STEPS)
        def _():
            stage_b(j + 1)

        @pl.when(j + 2 < STEPS)
        def _():
            stage_a(j + 2)

        @pl.when(j >= 1)
        def _():
            stage_d(j - 1)

        @pl.when(j >= 2)
        def _():
            stage_e(j - 2)

        return 0

    lax.fori_loop(0, STEPS, step, 0)

    for k in range(2):
        tiles = packed(jnp.sum(MH[k], axis=1, keepdims=True))
        for b in range(SLAB // BLK):
            MHS[k, 8 * b : 8 * b + 8, :] = tiles[b]
    for d in SIDES:
        cp_mh(d).start()
    for b in range(OWN // BLK):
        column = jnp.sum(M[b * BLK : (b + 1) * BLK, :], axis=1, keepdims=True)
        MT[8 * b : 8 * b + 8, :] = packed(column)[0]
    stage_d(STEPS - 1)
    for d in SIDES:
        cp_mh(d, True).wait_recv()
    MT[:24, :] += MHR[0]
    MT[72:96, :] += MHR[1]
    for d in ALL:
        cp_m(d).start()
    MR[y] = MT[span(24 * y, 24, 8), :]
    stage_e(STEPS - 2)
    for d in ALL:
        cp_m(d, True).wait_recv()

    def arrived(j, _):
        for d in ALL:
            cp_a(j, d, True).wait_recv()
        return 0

    lax.fori_loop(0, STEPS, arrived, 0)
    for b in range(SLAB // BLK):
        rows = slice(b * BLK, (b + 1) * BLK)
        tiles = slice(8 * b, 8 * b + 8)
        mean = (MR[0, tiles] + MR[1, tiles] + MR[2, tiles] + MR[3, tiles]) * (1.0 / WIDTH)
        r = RT[tiles, :]
        factor = unpacked(mean * (r * r))[:, :1]
        DH[rows, :] = (AF[rows, :].astype(f32) - HS[rows, :].astype(f32) * factor).astype(bf16)
    store = pltpu.make_async_copy(DH, dh_out, loc1.at[1])
    store.start()
    stage_e(STEPS - 1)
    store.wait()

    def last(j, _):
        for d in ALL:
            cp_att(j, d, True).wait_recv()
            cp_g2k(j, d, True).wait_recv()
            cp_g2v(j, d, True).wait_recv()
            for copy in (cp_h, cp_do, cp_tx, cp_ty, cp_tg, cp_att, cp_a, cp_rs, cp_g1k, cp_g1v, cp_g2k, cp_g2v):
                copy(j, d).wait_send()
        for d in SIDES:
            cp_halo(j, d).wait_send()
            cp_ah(j, d).wait_send()
        lo_att(j).wait()
        lo_g2k(j).wait()
        lo_g2v(j).wait()
        return 0

    lax.fori_loop(0, STEPS, last, 0)
    for d in ALL:
        cp_r(d).wait_send()
        cp_m(d).wait_send()
    for d in SIDES:
        cp_rh(d).wait_send()
        cp_mh(d).wait_send()


def query_bias(pattern, x):
    blocks = OWN // BLK
    reach = SLAB // BLK
    span_ = pattern.shape[1]
    rows = lax.dynamic_slice_in_dim(pattern, x * blocks, blocks, 0)
    first = jnp.arange(blocks, dtype=jnp.int32)[:, None]
    col = jnp.arange(BLK, dtype=jnp.int32)[None, :]
    offset = col - first
    onehot = offset[:, :, None] == jnp.arange(span_, dtype=jnp.int32)[None, None, :]
    picked = jnp.sum(jnp.where(onehot, rows[:, None, :], 0), axis=-1)
    globe = x * blocks - reach + col
    inside = (globe >= 0) & (globe < pattern.shape[0])
    allowed = ((picked > 0) & inside) | (col >= EXT // BLK)
    return jnp.repeat(jnp.where(allowed, 0.0, NEG).astype(bf16), BLK, axis=0)


def shifted(x, axis, by):
    peers = lax.axis_size(axis)
    pairs = [(i, i + by) for i in range(peers) if 0 <= i + by < peers]
    return lax.ppermute(x, axis, pairs)


def local(hidden, query_norm_gain, key_norm_gain, text_kv, holder, pattern, grad_out):
    x = lax.axis_index("seq") // NY
    qbias = query_bias(pattern, x)
    who = holder[0]
    select = jnp.concatenate([jnp.arange(NX) == who // NY, jnp.arange(NY) == who % NY])
    select = jnp.broadcast_to(select.astype(f32)[:, None], (NX + NY, NY * BLK))
    heads = WIDTH // HDIM
    any_spec = pl.BlockSpec(memory_space=pl.ANY)
    vmem = pl.BlockSpec(memory_space=pltpu.VMEM)

    def V(*shape, dtype=bf16):
        return pltpu.VMEM(shape, dtype)

    attended, grad_hidden, text_total = pl.pallas_call(
        kernel,
        out_shape=(
            jax.ShapeDtypeStruct((SLAB, WIDTH), bf16),
            jax.ShapeDtypeStruct((SLAB, WIDTH), bf16),
            jax.ShapeDtypeStruct((2, TXT, WIDTH), bf16),
        ),
        in_specs=[any_spec] * 3 + [vmem] * 4,
        out_specs=[any_spec] * 3,
        scratch_shapes=[
            V(SLAB, WIDTH),
            V(STEPS, EXT, BLK),
            V(STEPS, OWN, BLK),
            V(EXT // BLK * 8, BLK, dtype=f32),
            V(24, BLK, dtype=f32),
            V(EXT, BLK, dtype=f32),
            V(STEPS, NX, 2, BLK, NY * BLK),
            V(STEPS, 2, BLK, NY * BLK),
            V(STEPS, NY, 2, BLK, BLK),
            V(STEPS, 2, TXT, BLK),
            V(KEYS, 2 * BLK),
            V(BLK, KEYS),
            V(BLK + 16, KEYS),
            V(QT, 2 * BLK),
            V(NCHUNK, KC, QT, dtype=f32),
            V(NCHUNK, KC, QT),
            V(KEYS, BLK, dtype=f32),
            V(KEYS, BLK, dtype=f32),
            V(OWN, BLK, dtype=f32),
            V(STEPS, OWN, BLK),
            V(2, OWN, BLK, dtype=f32),
            V(STEPS, 2, SLAB, BLK),
            V(STEPS, 2, SLAB, BLK),
            V(STEPS, OWN, BLK),
            V(SLAB, WIDTH),
            V(OWN, BLK, dtype=f32),
            V(2, SLAB, BLK, dtype=f32),
            V(96, BLK, dtype=f32),
            V(2, 24, BLK, dtype=f32),
            V(2, 24, BLK, dtype=f32),
            V(NY, 24, BLK, dtype=f32),
            V(STEPS, 2, TXT, BLK),
            V(STEPS, NX, 2, BLK, BLK),
            V(STEPS, 2, BLK, BLK),
            V(STEPS, BLK, NY * BLK),
            V(STEPS, TXT, BLK),
            V(SLAB, WIDTH),
            pltpu.SemaphoreType.DMA((KINDS, STEPS, 8)),
            pltpu.SemaphoreType.DMA((KINDS, STEPS, 8)),
            pltpu.SemaphoreType.DMA((4, 4)),
            pltpu.SemaphoreType.DMA((4, 4)),
            pltpu.SemaphoreType.DMA((6, STEPS)),
            pltpu.SemaphoreType.DMA((2,)),
        ],
        compiler_params=pltpu.CompilerParams(
            collective_id=0, has_side_effects=True, vmem_limit_bytes=60 * 1024 * 1024
        ),
        cost_estimate=pl.CostEstimate(
            flops=24 * 10**9, bytes_accessed=40 * 10**6, transcendentals=12 * 10**6
        ),
        name="attention",
    )(
        hidden[0],
        grad_out[0],
        text_kv[0, 0],
        query_norm_gain.reshape(heads, HDIM),
        key_norm_gain.reshape(heads, HDIM),
        select,
        qbias,
    )
    upstream = shifted(grad_hidden, "section", -1)
    return (attended[None], upstream[None], text_total[None])


def solution(mesh):
    in_specs = (
        P("section", "seq", None),
        P("section", None),
        P("section", None),
        P("section", "seq", None, None, None),
        P("section"),
        P(),
        P("section", "seq", None),
    )
    out_specs = (
        P("section", "seq", None),
        P("section", "seq", None),
        P("section", None, None, None),
    )
    return jax.shard_map(local, mesh=mesh, in_specs=in_specs, out_specs=out_specs, check_vma=False)
```

```python
import jax
import jax.numpy as jnp
from jax import lax
from jax.experimental import pallas as pl
from jax.experimental.pallas import tpu as pltpu
from jax.sharding import PartitionSpec as P

HDIM = 128
BLK = 128
EPS = 1e-06
MESH = pl.DeviceIdType.MESH

NX = 4
NY = 4
SLAB = 384
TXT = 512
WIDTH = 2560
STEPS = 5
OWN = NY * SLAB
EXT = OWN + 2 * SLAB
KEYS = EXT + TXT
QT = 256
KC = 256
NCHUNK = 4 + TXT // KC
SCALE = HDIM ** (-0.5)
LOG2E = 1.4426950408889634
NEG = -1e30

(
    K_H,
    K_DO,
    K_TX,
    K_TY,
    K_TG,
    K_HALO,
    K_ATT,
    K_AH,
    K_A,
    K_RS,
    K_G1,
    K_G2,
) = range(12)
KINDS = 12
O_R, O_RH, O_MH, O_M, O_HU = range(5)

f32 = jnp.float32
bf16 = jnp.bfloat16


def dot_nn(a, b):
    return lax.dot_general(a, b, (((1,), (0,)), ((), ())), preferred_element_type=f32)


def dot_nt(a, b):
    return lax.dot_general(a, b, (((1,), (1,)), ((), ())), preferred_element_type=f32)


def block(k):
    return pl.ds(pl.multiple_of(k * BLK, BLK), BLK)


def span(start, size, unit):
    return pl.ds(pl.multiple_of(start, unit), size)


def packed(column):
    rows = column.shape[0]
    wide = jnp.broadcast_to(column, (rows, BLK))
    return [wide[b * BLK : (b + 1) * BLK].T[:8] for b in range(rows // BLK)]


def unpacked(tile):
    return jnp.broadcast_to(tile[:1], (BLK, BLK)).T


def kernel(
    hid, do_in, txt, gq_ref, gk_ref, sel_ref, qb_ref,
    att_out, dh_out, tg_out,
    HS, HU, RU, HX, DO, RTX, RT, RB, T1, TS, T2, T3, KA, KT, VT, QA, S, PB, DK, DV, DQ,
    ATT, AFS, AH, AHR, AO, AF, M, MH, MT, MHS, MHR, MR, TGP, TG1, TG2, TGY, TGX, DH,
    send, recv, once_send, once_recv, loc, loc1,
):
    seq = lax.axis_index("seq")
    section = lax.axis_index("section")
    sections = lax.axis_size("section")
    x = lax.div(seq, NY)
    y = lax.rem(seq, NY)

    def ry(d):
        return lax.rem(y + (d + NY), NY)

    def rx(d):
        return lax.rem(x + (d + NX), NX)

    def yid(d):
        return {"seq": x * NY + ry(d)}

    def xid(d):
        return {"seq": rx(d) * NY + y}

    def below(d):
        return {"seq": x * NY + ry(d), "section": lax.rem(section + (sections - 1), sections)}

    def above(d):
        return {"seq": x * NY + ry(d), "section": lax.rem(section + 1, sections)}

    def rc(src, dst, kind, j, d, dev):
        return pltpu.make_async_remote_copy(
            src_ref=src, dst_ref=dst, send_sem=send.at[kind, j, d],
            recv_sem=recv.at[kind, j, d], device_id=dev, device_id_type=MESH,
        )

    def rc1(src, dst, kind, d, dev):
        return pltpu.make_async_remote_copy(
            src_ref=src, dst_ref=dst, send_sem=once_send.at[kind, d],
            recv_sem=once_recv.at[kind, d], device_id=dev, device_id_type=MESH,
        )

    def hcol(j, yy):
        return block(NY * j + yy)

    def wide(j):
        return span(j * (NY * BLK), NY * BLK, NY * BLK)

    def slab(yy):
        return span(SLAB + SLAB * yy, SLAB, SLAB)

    def oslab(yy):
        return span(SLAB * yy, SLAB, SLAB)

    def cp_h(j, d, w=False):
        return rc(hid.at[:, hcol(j, ry(d))], HX.at[j, slab(ry(-d) if w else y), :], K_H, j, d, yid(d))

    def cp_do(j, d, w=False):
        return rc(do_in.at[:, hcol(j, ry(d))], DO.at[j, oslab(ry(-d) if w else y), :], K_DO, j, d, yid(d))

    def cp_tx(j, d, w=False):
        return rc(txt.at[:, block(rx(d)), wide(j)], T1.at[j, rx(-d) if w else x], K_TX, j, d, xid(d))

    def cp_ty(j, d, w=False):
        return rc(TS.at[j, :, :, block(ry(d))], T2.at[j, ry(-d) if w else y], K_TY, j, d, yid(d))

    def cp_tg(j, d, w=False):
        return rc(T3.at[j, :, block(x), :], T3.at[j, :, block(rx(-d) if w else x), :], K_TG, j, d, xid(d))

    def cp_halo(j, d, w=False):
        if d == 1:
            return rc(HX.at[j, pl.ds(OWN, SLAB), :], HX.at[j, pl.ds(0, SLAB), :], K_HALO, j, 1, xid(1))
        return rc(HX.at[j, pl.ds(SLAB, SLAB), :], HX.at[j, pl.ds(OWN + SLAB, SLAB), :], K_HALO, j, 3, xid(3))

    def cp_att(j, d, w=False):
        return rc(ATT.at[j, oslab(ry(d)), :], att_out.at[:, hcol(j, ry(-d) if w else y)], K_ATT, j, d, yid(d))

    def cp_ah(j, d, w=False):
        k = 1 if d == 1 else 0
        return rc(AH.at[j, k], AHR.at[j, 1 - k], K_AH, j, d, xid(d))

    def cp_a(j, d, w=False):
        return rc(AO.at[j, oslab(ry(d)), :], AF.at[:, hcol(j, ry(-d) if w else y)], K_A, j, d, below(d))

    def cp_rs(j, d, w=False):
        return rc(TGP.at[j, :, block(rx(d)), :], TG1.at[j, rx(-d) if w else x], K_RS, j, d, xid(d))

    def cp_g1k(j, d, w=False):
        return rc(TG2.at[j, 0], TGY.at[j, :, block(ry(-d) if w else y)], K_G1, j, d, yid(d))

    def cp_g1v(j, d, w=False):
        return rc(TG2.at[j, 1], TGX.at[j, block(rx(-d) if w else x), :], K_G1, j, 4 + d, xid(d))

    def cp_g2k(j, d, w=False):
        return rc(TGY.at[j], tg_out.at[0, block(rx(-d) if w else x), wide(j)], K_G2, j, d, xid(d))

    def cp_g2v(j, d, w=False):
        return rc(TGX.at[j], tg_out.at[1, :, hcol(j, ry(-d) if w else y)], K_G2, j, 4 + d, yid(d))

    def cp_r(d, w=False):
        return rc1(RT, RTX.at[span(24 + 24 * (ry(-d) if w else y), 24, 8), :], O_R, d, yid(d))

    def cp_rh(d, w=False):
        if d == 1:
            return rc1(RTX.at[pl.ds(96, 24), :], RTX.at[pl.ds(0, 24), :], O_RH, 1, xid(1))
        return rc1(RTX.at[pl.ds(24, 24), :], RTX.at[pl.ds(120, 24), :], O_RH, 3, xid(3))

    def cp_mh(d, w=False):
        k = 1 if d == 1 else 0
        return rc1(MHS.at[k], MHR.at[1 - k], O_MH, d, xid(d))

    def cp_m(d, w=False):
        return rc1(MT.at[span(24 * ry(d), 24, 8), :], MR.at[ry(-d) if w else y], O_M, d, below(d))

    def cp_hu():
        return rc1(hid, HU, O_HU, 0, below(0))

    def cp_ru():
        return rc1(RT, RU, O_HU, 1, below(0))

    def lo_h(j):
        return pltpu.make_async_copy(hid.at[:, hcol(j, y)], HX.at[j, slab(y), :], loc.at[0, j])

    def lo_do(j):
        return pltpu.make_async_copy(do_in.at[:, hcol(j, y)], DO.at[j, oslab(y), :], loc.at[1, j])

    def lo_tx(j):
        return pltpu.make_async_copy(txt.at[:, block(x), wide(j)], T1.at[j, x], loc.at[2, j])

    def lo_att(j):
        return pltpu.make_async_copy(ATT.at[j, oslab(y), :], att_out.at[:, hcol(j, y)], loc.at[3, j])

    def lo_g2k(j):
        return pltpu.make_async_copy(TGY.at[j], tg_out.at[0, block(x), wide(j)], loc.at[4, j])

    def lo_g2v(j):
        return pltpu.make_async_copy(TGX.at[j], tg_out.at[1, :, hcol(j, y)], loc.at[5, j])

    ALL = (1, 3, 2)
    FOUR = (0, 1, 3, 2)
    SIDES = (1, 3)

    def front(j):
        for d in ALL:
            cp_tx(j, d).start()
            cp_h(j, d).start()
        for d in ALL:
            cp_do(j, d).start()

    def stage_a(j):
        lo_tx(j).wait()
        for d in ALL:
            cp_tx(j, d, True).wait_recv()
        for kv in range(2):
            part = jnp.zeros((BLK, NY * BLK), f32)
            for k in range(NX):
                part = part + T1[j, k, kv].astype(f32) * sel_ref[k : k + 1, :]
            TS[j, kv] = part.astype(bf16)
        T2[j, y] = TS[j, :, :, block(y)]
        for d in ALL:
            cp_ty(j, d).start()
        lo_h(j).wait()
        for d in ALL:
            cp_h(j, d, True).wait_recv()
        for d in SIDES:
            cp_halo(j, d).start()

    def stage_b(j):
        for d in ALL:
            cp_ty(j, d, True).wait_recv()
        for kv in range(2):
            part = jnp.zeros((BLK, BLK), f32)
            for k in range(NY):
                part = part + T2[j, k, kv].astype(f32) * sel_ref[NX + k : NX + k + 1, :BLK]
            T3[j, kv, block(x), :] = part.astype(bf16)
        for d in ALL:
            cp_tg(j, d).start()

    def stage_c(j):
        for d in SIDES:
            cp_halo(j, d, True).wait_recv()
        lo_do(j).wait()
        for d in ALL:
            cp_do(j, d, True).wait_recv()
            cp_tg(j, d, True).wait_recv()
        head = NY * j + y
        gq = gq_ref[pl.ds(head, 1), :]
        gk = gk_ref[pl.ds(head, 1), :]
        par = lax.rem(j, 2)

        def prep(b, _):
            rows = block(b)
            h = HX[j, rows, :].astype(f32)
            kn = (h * RB[rows, :]) * gk
            KA[rows, :BLK] = kn.astype(bf16)
            KT[:, rows] = kn.T.astype(bf16)
            VT[:BLK, rows] = h.T.astype(bf16)
            return 0

        lax.fori_loop(0, EXT // BLK, prep, 0)
        for b in range(TXT // BLK):
            rows = slice(EXT + b * BLK, EXT + (b + 1) * BLK)
            kn = T3[j, 0, b * BLK : (b + 1) * BLK, :]
            KA[rows, :BLK] = kn
            KT[:, rows] = kn.astype(f32).T.astype(bf16)
            VT[:BLK, rows] = T3[j, 1, b * BLK : (b + 1) * BLK, :].astype(f32).T.astype(bf16)

        def clear(b, _):
            rows = span(b * KC, KC, KC)
            DK[rows, :] = jnp.zeros((KC, BLK), f32)
            DV[rows, :] = jnp.zeros((KC, BLK), f32)
            return 0

        lax.fori_loop(0, KEYS // KC, clear, 0)

        def tile(u, _):
            q0 = u * QT
            qrows = span(q0, QT, QT)
            erows = span(SLAB + q0, QT, BLK)
            h = HX[j, erows, :].astype(f32)
            qn = ((h * RB[erows, :]) * gq).astype(bf16)
            QA[:, :BLK] = qn
            QA[:, BLK:] = qb_ref[qrows, :]
            qa = QA[...]
            chunks = [span(q0 + KC * c, KC, KC) for c in range(4)]
            chunks += [pl.ds(EXT + KC * c, KC) for c in range(TXT // KC)]
            top = None
            for c in range(NCHUNK):
                s = dot_nt(KA[chunks[c], :], qa)
                S[c] = s
                high = jnp.max(s, axis=0, keepdims=True)
                top = high if top is None else jnp.maximum(top, high)
            top = top * (SCALE * LOG2E)
            ot = None
            for c in range(NCHUNK):
                p = jnp.exp2(S[c] * (SCALE * LOG2E) - top).astype(bf16)
                PB[c] = p
                term = dot_nn(VT[:, chunks[c]], p)
                ot = term if ot is None else ot + term
            inv = 1.0 / ot[BLK : BLK + 1, :]
            o = ot[:BLK, :] * inv
            dt = DO[j, qrows, :].astype(f32).T
            delta = jnp.sum(dt * o, axis=0, keepdims=True) * inv
            dts = (dt * inv).astype(bf16)
            ATT[j, qrows, :] = o.T.astype(bf16)
            dq = None
            for c in range(NCHUNK):
                if c < 4:
                    v = HX[j, chunks[c], :]
                else:
                    v = T3[j, 1, (c - 4) * KC : (c - 3) * KC, :]
                p = PB[c]
                dp = dot_nn(v, dts)
                ds = (p.astype(f32) * (dp - delta)).astype(bf16)
                DV[chunks[c], :] += dot_nt(p, dts)
                DK[chunks[c], :] += dot_nn(ds, qn)
                term = dot_nn(KT[:, chunks[c]], ds)
                dq = term if dq is None else dq + term
            DQ[qrows, :] = dq.T
            return 0

        lax.fori_loop(0, OWN // QT, tile, 0)

        for d in ALL:
            cp_att(j, d).start()
        lo_att(j).start()

        for k in range(2):
            rows = slice(k * (OWN + SLAB), k * (OWN + SLAB) + SLAB)
            r = RB[rows, :]
            t = (gk * DK[rows, :]) * SCALE
            AH[j, k] = (DV[rows, :] + r * t).astype(bf16)
            MH[k] += (HX[j, rows, :].astype(f32) * r) * t
        for d in SIDES:
            cp_ah(j, d).start()
        TGP[j, 0] = (DK[EXT:, :] * SCALE).astype(bf16)
        TGP[j, 1] = DV[EXT:, :].astype(bf16)
        TG1[j, x] = TGP[j, :, block(x), :]
        for d in ALL:
            cp_rs(j, d).start()

        def own(i, _):
            rows = slab(i)
            qrows = oslab(i)
            r = RB[rows, :]
            t = (gq * DQ[qrows, :] + gk * DK[rows, :]) * SCALE
            AFS[par, qrows, :] = DV[rows, :] + r * t
            M[qrows, :] += (HX[j, rows, :].astype(f32) * r) * t
            return 0

        lax.fori_loop(0, NY, own, 0)

    def stage_d(j):
        par = lax.rem(j, 2)
        for d in SIDES:
            cp_ah(j, d, True).wait_recv()
        for i in range(NY):
            rows = slice(i * SLAB, (i + 1) * SLAB)
            a = AFS[par, rows, :]
            if i == 0:
                a = a + AHR[j, 0].astype(f32)
            if i == NY - 1:
                a = a + AHR[j, 1].astype(f32)
            AO[j, rows, :] = a.astype(bf16)
        for d in FOUR:
            cp_a(j, d).start()
        for d in ALL:
            cp_rs(j, d, True).wait_recv()
        for kv in range(2):
            total = TG1[j, 0, kv].astype(f32)
            for k in range(1, NX):
                total = total + TG1[j, k, kv].astype(f32)
            TG2[j, kv] = total.astype(bf16)
        TGY[j, :, block(y)] = TG2[j, 0]
        TGX[j, block(x), :] = TG2[j, 1]
        for d in ALL:
            cp_g1k(j, d).start()
            cp_g1v(j, d).start()

    def stage_e(j):
        for d in ALL:
            cp_g1k(j, d, True).wait_recv()
            cp_g1v(j, d, True).wait_recv()
        for d in ALL:
            cp_g2k(j, d).start()
            cp_g2v(j, d).start()
        lo_g2k(j).start()
        lo_g2v(j).start()

    barrier = pltpu.get_barrier_semaphore()
    for d in ALL:
        pl.semaphore_signal(barrier, inc=1, device_id=yid(d), device_id_type=MESH)
        pl.semaphore_signal(barrier, inc=1, device_id=xid(d), device_id_type=MESH)
    for d in FOUR:
        pl.semaphore_signal(barrier, inc=1, device_id=above(d), device_id_type=MESH)
    load = pltpu.make_async_copy(hid, HS, loc1.at[0])
    load.start()

    def first_local(j, _):
        lo_h(j).start()
        lo_tx(j).start()
        lo_do(j).start()
        return 0

    lax.fori_loop(0, STEPS, first_local, 0)
    pl.semaphore_wait(barrier, 10)

    front(0)
    cp_hu().start()

    lane = lax.broadcasted_iota(jnp.int32, (BLK, BLK), 1)

    def marks(b, _):
        KA[block(b), BLK:] = jnp.where(lane == b, 1.0, 0.0).astype(bf16)
        return 0

    lax.fori_loop(0, EXT // BLK, marks, 0)
    KA[EXT:, BLK:] = jnp.zeros((TXT, BLK), bf16)
    VT[BLK:, :] = jnp.ones((16, KEYS), bf16)

    def clear_m(i, _):
        M[oslab(i), :] = jnp.zeros((SLAB, BLK), f32)
        return 0

    lax.fori_loop(0, NY, clear_m, 0)
    for k in range(2):
        MH[k] = jnp.zeros((SLAB, BLK), f32)

    load.wait()

    for b in range(SLAB // BLK):
        h = HS[b * BLK : (b + 1) * BLK, :].astype(f32)
        mean = jnp.sum(h * h, axis=1, keepdims=True) * (1.0 / WIDTH)
        RT[8 * b : 8 * b + 8, :] = packed(lax.rsqrt(mean + EPS))[0]
    for d in ALL:
        cp_r(d).start()
    cp_ru().start()
    RTX[span(24 + 24 * y, 24, 8), :] = RT[...]
    for d in ALL:
        cp_r(d, True).wait_recv()
    for d in SIDES:
        cp_rh(d).start()
    for d in SIDES:
        cp_rh(d, True).wait_recv()
    stage_a(0)
    front(1)
    for b in range(EXT // BLK):
        RB[b * BLK : (b + 1) * BLK, :] = unpacked(RTX[8 * b : 8 * b + 8, :])
    stage_b(0)
    front(2)
    stage_a(1)

    def step(j, _):
        stage_c(j)

        @pl.when(j + 3 < STEPS)
        def _():
            front(j + 3)

        @pl.when(j + 1 < STEPS)
        def _():
            stage_b(j + 1)

        @pl.when(j + 2 < STEPS)
        def _():
            stage_a(j + 2)

        @pl.when(j >= 1)
        def _():
            stage_d(j - 1)

        @pl.when(j >= 2)
        def _():
            stage_e(j - 2)

        return 0

    lax.fori_loop(0, STEPS, step, 0)

    for k in range(2):
        tiles = packed(jnp.sum(MH[k], axis=1, keepdims=True))
        for b in range(SLAB // BLK):
            MHS[k, 8 * b : 8 * b + 8, :] = tiles[b]
    for d in SIDES:
        cp_mh(d).start()
    for b in range(OWN // BLK):
        column = jnp.sum(M[b * BLK : (b + 1) * BLK, :], axis=1, keepdims=True)
        MT[8 * b : 8 * b + 8, :] = packed(column)[0]
    stage_d(STEPS - 1)
    for d in SIDES:
        cp_mh(d, True).wait_recv()
    MT[:24, :] += MHR[0]
    MT[72:96, :] += MHR[1]
    for d in FOUR:
        cp_m(d).start()
    stage_e(STEPS - 2)
    cp_hu().wait_recv()
    cp_ru().wait_recv()
    for d in FOUR:
        cp_m(d, True).wait_recv()

    def arrived(j, _):
        for d in FOUR:
            cp_a(j, d, True).wait_recv()
        return 0

    lax.fori_loop(0, STEPS, arrived, 0)
    for b in range(SLAB // BLK):
        rows = slice(b * BLK, (b + 1) * BLK)
        tiles = slice(8 * b, 8 * b + 8)
        mean = (MR[0, tiles] + MR[1, tiles] + MR[2, tiles] + MR[3, tiles]) * (1.0 / WIDTH)
        r = RU[tiles, :]
        factor = unpacked(mean * (r * r))[:, :1]
        grad = AF[rows, :].astype(f32) - HU[rows, :].astype(f32) * factor
        DH[rows, :] = jnp.where(section < sections - 1, grad, 0.0).astype(bf16)
    store = pltpu.make_async_copy(DH, dh_out, loc1.at[1])
    store.start()
    stage_e(STEPS - 1)
    store.wait()

    def last(j, _):
        for d in ALL:
            cp_att(j, d, True).wait_recv()
            cp_g2k(j, d, True).wait_recv()
            cp_g2v(j, d, True).wait_recv()
            for copy in (cp_h, cp_do, cp_tx, cp_ty, cp_tg, cp_att, cp_rs, cp_g1k, cp_g1v, cp_g2k, cp_g2v):
                copy(j, d).wait_send()
        for d in FOUR:
            cp_a(j, d).wait_send()
        for d in SIDES:
            cp_halo(j, d).wait_send()
            cp_ah(j, d).wait_send()
        lo_att(j).wait()
        lo_g2k(j).wait()
        lo_g2v(j).wait()
        return 0

    lax.fori_loop(0, STEPS, last, 0)
    for d in ALL:
        cp_r(d).wait_send()
    for d in FOUR:
        cp_m(d).wait_send()
    cp_hu().wait_send()
    cp_ru().wait_send()
    for d in SIDES:
        cp_rh(d).wait_send()
        cp_mh(d).wait_send()


def query_bias(pattern, x):
    blocks = OWN // BLK
    reach = SLAB // BLK
    span_ = pattern.shape[1]
    rows = lax.dynamic_slice_in_dim(pattern, x * blocks, blocks, 0)
    first = jnp.arange(blocks, dtype=jnp.int32)[:, None]
    col = jnp.arange(BLK, dtype=jnp.int32)[None, :]
    offset = col - first
    onehot = offset[:, :, None] == jnp.arange(span_, dtype=jnp.int32)[None, None, :]
    picked = jnp.sum(jnp.where(onehot, rows[:, None, :], 0), axis=-1)
    globe = x * blocks - reach + col
    inside = (globe >= 0) & (globe < pattern.shape[0])
    allowed = ((picked > 0) & inside) | (col >= EXT // BLK)
    return jnp.repeat(jnp.where(allowed, 0.0, NEG).astype(bf16), BLK, axis=0)


def local(hidden, query_norm_gain, key_norm_gain, text_kv, holder, pattern, grad_out):
    x = lax.axis_index("seq") // NY
    qbias = query_bias(pattern, x)
    who = holder[0]
    select = jnp.concatenate([jnp.arange(NX) == who // NY, jnp.arange(NY) == who % NY])
    select = jnp.broadcast_to(select.astype(f32)[:, None], (NX + NY, NY * BLK))
    heads = WIDTH // HDIM
    any_spec = pl.BlockSpec(memory_space=pl.ANY)
    vmem = pl.BlockSpec(memory_space=pltpu.VMEM)

    def V(*shape, dtype=bf16):
        return pltpu.VMEM(shape, dtype)

    attended, upstream, text_total = pl.pallas_call(
        kernel,
        out_shape=(
            jax.ShapeDtypeStruct((SLAB, WIDTH), bf16),
            jax.ShapeDtypeStruct((SLAB, WIDTH), bf16),
            jax.ShapeDtypeStruct((2, TXT, WIDTH), bf16),
        ),
        in_specs=[any_spec] * 3 + [vmem] * 4,
        out_specs=[any_spec] * 3,
        scratch_shapes=[
            V(SLAB, WIDTH),
            V(SLAB, WIDTH),
            V(24, BLK, dtype=f32),
            V(STEPS, EXT, BLK),
            V(STEPS, OWN, BLK),
            V(EXT // BLK * 8, BLK, dtype=f32),
            V(24, BLK, dtype=f32),
            V(EXT, BLK, dtype=f32),
            V(STEPS, NX, 2, BLK, NY * BLK),
            V(STEPS, 2, BLK, NY * BLK),
            V(STEPS, NY, 2, BLK, BLK),
            V(STEPS, 2, TXT, BLK),
            V(KEYS, 2 * BLK),
            V(BLK, KEYS),
            V(BLK + 16, KEYS),
            V(QT, 2 * BLK),
            V(NCHUNK, KC, QT, dtype=f32),
            V(NCHUNK, KC, QT),
            V(KEYS, BLK, dtype=f32),
            V(KEYS, BLK, dtype=f32),
            V(OWN, BLK, dtype=f32),
            V(STEPS, OWN, BLK),
            V(2, OWN, BLK, dtype=f32),
            V(STEPS, 2, SLAB, BLK),
            V(STEPS, 2, SLAB, BLK),
            V(STEPS, OWN, BLK),
            V(SLAB, WIDTH),
            V(OWN, BLK, dtype=f32),
            V(2, SLAB, BLK, dtype=f32),
            V(96, BLK, dtype=f32),
            V(2, 24, BLK, dtype=f32),
            V(2, 24, BLK, dtype=f32),
            V(NY, 24, BLK, dtype=f32),
            V(STEPS, 2, TXT, BLK),
            V(STEPS, NX, 2, BLK, BLK),
            V(STEPS, 2, BLK, BLK),
            V(STEPS, BLK, NY * BLK),
            V(STEPS, TXT, BLK),
            V(SLAB, WIDTH),
            pltpu.SemaphoreType.DMA((KINDS, STEPS, 8)),
            pltpu.SemaphoreType.DMA((KINDS, STEPS, 8)),
            pltpu.SemaphoreType.DMA((5, 4)),
            pltpu.SemaphoreType.DMA((5, 4)),
            pltpu.SemaphoreType.DMA((6, STEPS)),
            pltpu.SemaphoreType.DMA((2,)),
        ],
        compiler_params=pltpu.CompilerParams(
            collective_id=0, has_side_effects=True, vmem_limit_bytes=60 * 1024 * 1024
        ),
        cost_estimate=pl.CostEstimate(
            flops=24 * 10**9, bytes_accessed=40 * 10**6, transcendentals=12 * 10**6
        ),
        name="attention",
    )(
        hidden[0],
        grad_out[0],
        text_kv[0, 0],
        query_norm_gain.reshape(heads, HDIM),
        key_norm_gain.reshape(heads, HDIM),
        select,
        qbias,
    )
    return (attended[None], upstream[None], text_total[None])


def solution(mesh):
    in_specs = (
        P("section", "seq", None),
        P("section", None),
        P("section", None),
        P("section", "seq", None, None, None),
        P("section"),
        P(),
        P("section", "seq", None),
    )
    out_specs = (
        P("section", "seq", None),
        P("section", "seq", None),
        P("section", None, None, None),
    )
    return jax.shard_map(local, mesh=mesh, in_specs=in_specs, out_specs=out_specs, check_vma=False)
```

```python
import jax
import jax.numpy as jnp
from jax import lax
from jax.experimental import pallas as pl
from jax.experimental.pallas import tpu as pltpu
from jax.sharding import PartitionSpec as P

HDIM = 128
BLK = 128
EPS = 1e-06
MESH = pl.DeviceIdType.MESH

NX = 4
NY = 4
SLAB = 384
TXT = 512
WIDTH = 2560
STEPS = 5
OWN = NY * SLAB
EXT = OWN + 2 * SLAB
KEYS = EXT + TXT
QT = 256
KC = 256
NCHUNK = 4 + TXT // KC
SCALE = HDIM ** (-0.5)
LOG2E = 1.4426950408889634
NEG = -1e30

(
    K_H,
    K_DO,
    K_TX,
    K_TY,
    K_TG,
    K_HALO,
    K_ATT,
    K_AH,
    K_A,
    K_RS,
    K_G1,
    K_G2,
) = range(12)
KINDS = 12
O_R, O_RH, O_MH, O_M, O_HU = range(5)

f32 = jnp.float32
bf16 = jnp.bfloat16


def dot_nn(a, b):
    return lax.dot_general(a, b, (((1,), (0,)), ((), ())), preferred_element_type=f32)


def dot_nt(a, b):
    return lax.dot_general(a, b, (((1,), (1,)), ((), ())), preferred_element_type=f32)


def woven(*parts):
    parts = list(parts)
    while parts:
        for part in list(parts):
            if next(part, True):
                parts.remove(part)


def block(k):
    return pl.ds(pl.multiple_of(k * BLK, BLK), BLK)


def span(start, size, unit):
    return pl.ds(pl.multiple_of(start, unit), size)


def packed(column):
    rows = column.shape[0]
    wide = jnp.broadcast_to(column, (rows, BLK))
    return [wide[b * BLK : (b + 1) * BLK].T[:8] for b in range(rows // BLK)]


def unpacked(tile):
    return jnp.broadcast_to(tile[:1], (BLK, BLK)).T


def kernel(
    hid, do_in, txt, gq_ref, gk_ref, sel_ref, qb_ref,
    att_out, dh_out, tg_out,
    HS, HU, RU, HX, DO, RTX, RT, RB, T1, TS, T2, T3, KA, KT, VT, QA0, QA1, S, PB0, PB1, DTS0, DTS1, DL0, DL1, DK, DV, DQ,
    ATT, AFS, AH, AHR, AO, AF, M, MH, MT, MHS, MHR, MR, TGP, TG1, TG2, TGY, TGX, DH,
    send, recv, once_send, once_recv, loc, loc1,
):
    QA, PB, DTS, DL = (QA0, QA1), (PB0, PB1), (DTS0, DTS1), (DL0, DL1)
    seq = lax.axis_index("seq")
    section = lax.axis_index("section")
    sections = lax.axis_size("section")
    x = lax.div(seq, NY)
    y = lax.rem(seq, NY)

    def ry(d):
        return lax.rem(y + (d + NY), NY)

    def rx(d):
        return lax.rem(x + (d + NX), NX)

    def yid(d):
        return {"seq": x * NY + ry(d)}

    def xid(d):
        return {"seq": rx(d) * NY + y}

    def below(d):
        return {"seq": x * NY + ry(d), "section": lax.rem(section + (sections - 1), sections)}

    def above(d):
        return {"seq": x * NY + ry(d), "section": lax.rem(section + 1, sections)}

    def rc(src, dst, kind, j, d, dev):
        return pltpu.make_async_remote_copy(
            src_ref=src, dst_ref=dst, send_sem=send.at[kind, j, d],
            recv_sem=recv.at[kind, j, d], device_id=dev, device_id_type=MESH,
        )

    def rc1(src, dst, kind, d, dev):
        return pltpu.make_async_remote_copy(
            src_ref=src, dst_ref=dst, send_sem=once_send.at[kind, d],
            recv_sem=once_recv.at[kind, d], device_id=dev, device_id_type=MESH,
        )

    def hcol(j, yy):
        return block(NY * j + yy)

    def wide(j):
        return span(j * (NY * BLK), NY * BLK, NY * BLK)

    def slab(yy):
        return span(SLAB + SLAB * yy, SLAB, SLAB)

    def oslab(yy):
        return span(SLAB * yy, SLAB, SLAB)

    def cp_h(j, d, w=False):
        return rc(hid.at[:, hcol(j, ry(d))], HX.at[j, slab(ry(-d) if w else y), :], K_H, j, d, yid(d))

    def cp_do(j, d, w=False):
        return rc(do_in.at[:, hcol(j, ry(d))], DO.at[j, oslab(ry(-d) if w else y), :], K_DO, j, d, yid(d))

    def cp_tx(j, d, w=False):
        return rc(txt.at[:, block(rx(d)), wide(j)], T1.at[j, rx(-d) if w else x], K_TX, j, d, xid(d))

    def cp_ty(j, d, w=False):
        return rc(TS.at[j, :, :, block(ry(d))], T2.at[j, ry(-d) if w else y], K_TY, j, d, yid(d))

    def cp_tg(j, d, w=False):
        return rc(T3.at[j, :, block(x), :], T3.at[j, :, block(rx(-d) if w else x), :], K_TG, j, d, xid(d))

    def cp_halo(j, d, w=False):
        if d == 1:
            return rc(HX.at[j, pl.ds(OWN, SLAB), :], HX.at[j, pl.ds(0, SLAB), :], K_HALO, j, 1, xid(1))
        return rc(HX.at[j, pl.ds(SLAB, SLAB), :], HX.at[j, pl.ds(OWN + SLAB, SLAB), :], K_HALO, j, 3, xid(3))

    def cp_att(j, d, w=False):
        return rc(ATT.at[j, oslab(ry(d)), :], att_out.at[:, hcol(j, ry(-d) if w else y)], K_ATT, j, d, yid(d))

    def cp_ah(j, d, w=False):
        k = 1 if d == 1 else 0
        return rc(AH.at[j, k], AHR.at[j, 1 - k], K_AH, j, d, xid(d))

    def cp_a(j, d, w=False):
        return rc(AO.at[j, oslab(ry(d)), :], AF.at[:, hcol(j, ry(-d) if w else y)], K_A, j, d, below(d))

    def cp_rs(j, d, w=False):
        return rc(TGP.at[j, :, block(rx(d)), :], TG1.at[j, rx(-d) if w else x], K_RS, j, d, xid(d))

    def cp_g1k(j, d, w=False):
        return rc(TG2.at[j, 0], TGY.at[j, :, block(ry(-d) if w else y)], K_G1, j, d, yid(d))

    def cp_g1v(j, d, w=False):
        return rc(TG2.at[j, 1], TGX.at[j, block(rx(-d) if w else x), :], K_G1, j, 4 + d, xid(d))

    def cp_g2k(j, d, w=False):
        return rc(TGY.at[j], tg_out.at[0, block(rx(-d) if w else x), wide(j)], K_G2, j, d, xid(d))

    def cp_g2v(j, d, w=False):
        return rc(TGX.at[j], tg_out.at[1, :, hcol(j, ry(-d) if w else y)], K_G2, j, 4 + d, yid(d))

    def cp_r(d, w=False):
        return rc1(RT, RTX.at[span(24 + 24 * (ry(-d) if w else y), 24, 8), :], O_R, d, yid(d))

    def cp_rh(d, w=False):
        if d == 1:
            return rc1(RTX.at[pl.ds(96, 24), :], RTX.at[pl.ds(0, 24), :], O_RH, 1, xid(1))
        return rc1(RTX.at[pl.ds(24, 24), :], RTX.at[pl.ds(120, 24), :], O_RH, 3, xid(3))

    def cp_mh(d, w=False):
        k = 1 if d == 1 else 0
        return rc1(MHS.at[k], MHR.at[1 - k], O_MH, d, xid(d))

    def cp_m(d, w=False):
        return rc1(MT.at[span(24 * ry(d), 24, 8), :], MR.at[ry(-d) if w else y], O_M, d, below(d))

    def cp_hu():
        return rc1(hid, HU, O_HU, 0, below(0))

    def cp_ru():
        return rc1(RT, RU, O_HU, 1, below(0))

    def lo_h(j):
        return pltpu.make_async_copy(hid.at[:, hcol(j, y)], HX.at[j, slab(y), :], loc.at[0, j])

    def lo_do(j):
        return pltpu.make_async_copy(do_in.at[:, hcol(j, y)], DO.at[j, oslab(y), :], loc.at[1, j])

    def lo_tx(j):
        return pltpu.make_async_copy(txt.at[:, block(x), wide(j)], T1.at[j, x], loc.at[2, j])

    def lo_att(j):
        return pltpu.make_async_copy(ATT.at[j, oslab(y), :], att_out.at[:, hcol(j, y)], loc.at[3, j])

    def lo_g2k(j):
        return pltpu.make_async_copy(TGY.at[j], tg_out.at[0, block(x), wide(j)], loc.at[4, j])

    def lo_g2v(j):
        return pltpu.make_async_copy(TGX.at[j], tg_out.at[1, :, hcol(j, y)], loc.at[5, j])

    ALL = (1, 3, 2)
    FOUR = (0, 1, 3, 2)
    SIDES = (1, 3)

    def front(j):
        for d in ALL:
            cp_tx(j, d).start()
            cp_h(j, d).start()
        for d in ALL:
            cp_do(j, d).start()

    def stage_a(j):
        lo_tx(j).wait()
        for d in ALL:
            cp_tx(j, d, True).wait_recv()
        for kv in range(2):
            part = jnp.zeros((BLK, NY * BLK), f32)
            for k in range(NX):
                part = part + T1[j, k, kv].astype(f32) * sel_ref[k : k + 1, :]
            TS[j, kv] = part.astype(bf16)
        T2[j, y] = TS[j, :, :, block(y)]
        for d in ALL:
            cp_ty(j, d).start()
        lo_h(j).wait()
        for d in ALL:
            cp_h(j, d, True).wait_recv()
        for d in SIDES:
            cp_halo(j, d).start()

    def stage_b(j):
        for d in ALL:
            cp_ty(j, d, True).wait_recv()
        for kv in range(2):
            part = jnp.zeros((BLK, BLK), f32)
            for k in range(NY):
                part = part + T2[j, k, kv].astype(f32) * sel_ref[NX + k : NX + k + 1, :BLK]
            T3[j, kv, block(x), :] = part.astype(bf16)
        for d in ALL:
            cp_tg(j, d).start()

    def stage_c(j, between):
        for d in SIDES:
            cp_halo(j, d, True).wait_recv()
        lo_do(j).wait()
        for d in ALL:
            cp_do(j, d, True).wait_recv()
            cp_tg(j, d, True).wait_recv()
        head = NY * j + y
        gq = gq_ref[pl.ds(head, 1), :]
        gk = gk_ref[pl.ds(head, 1), :]
        par = lax.rem(j, 2)

        def prep(b, _):
            rows = block(b)
            h = HX[j, rows, :].astype(f32)
            kn = (h * RB[rows, :]) * gk
            KA[rows, :BLK] = kn.astype(bf16)
            KT[:, rows] = kn.astype(bf16).T
            VT[:BLK, rows] = HX[j, rows, :].T
            return 0

        lax.fori_loop(0, EXT // BLK, prep, 0)
        for b in range(TXT // BLK):
            rows = slice(EXT + b * BLK, EXT + (b + 1) * BLK)
            kn = T3[j, 0, b * BLK : (b + 1) * BLK, :]
            KA[rows, :BLK] = kn
            KT[:, rows] = kn.T
            VT[:BLK, rows] = T3[j, 1, b * BLK : (b + 1) * BLK, :].T

        def clear(b, _):
            rows = span(b * KC, KC, KC)
            DK[rows, :] = jnp.zeros((KC, BLK), f32)
            DV[rows, :] = jnp.zeros((KC, BLK), f32)
            return 0

        lax.fori_loop(0, KEYS // KC, clear, 0)

        def chunks_of(q0):
            chunks = [span(q0 + KC * c, KC, KC) for c in range(4)]
            return chunks + [pl.ds(EXT + KC * c, KC) for c in range(TXT // KC)]

        def forward(u, k):
            q0 = u * QT
            qrows = span(q0, QT, QT)
            erows = span(SLAB + q0, QT, BLK)
            h = HX[j, erows, :].astype(f32)
            QA[k][:, :BLK] = ((h * RB[erows, :]) * gq).astype(bf16)
            for b in range(QT // BLK):
                bias = qb_ref[pl.ds(u * (QT // BLK) + b, 1), :].astype(bf16)
                QA[k][b * BLK : (b + 1) * BLK, BLK:] = jnp.broadcast_to(bias, (BLK, BLK))
            qa = QA[k][...]
            chunks = chunks_of(q0)
            top = None
            for c in range(NCHUNK):
                s = dot_nt(KA[chunks[c], :], qa)
                S[c] = s
                high = jnp.max(s, axis=0, keepdims=True)
                top = high if top is None else jnp.maximum(top, high)
                yield
            top = top * (SCALE * LOG2E)
            dt = DO[j, qrows, :].astype(f32).T
            ot = None
            for c in range(NCHUNK):
                p = jnp.exp2(S[c] * (SCALE * LOG2E) - top).astype(bf16)
                PB[k][c] = p
                term = dot_nn(VT[:, chunks[c]], p)
                ot = term if ot is None else ot + term
                yield
            inv = 1.0 / ot[BLK : BLK + 1, :]
            o = ot[:BLK, :] * inv
            delta = jnp.sum(dt * o, axis=0, keepdims=True) * inv
            DTS[k][...] = (dt * inv).astype(bf16)
            DL[k][...] = jnp.broadcast_to(delta, (8, QT))
            ATT[j, qrows, :] = o.T.astype(bf16)

        def backward(u, k):
            q0 = u * QT
            chunks = chunks_of(q0)
            dts = DTS[k][...]
            delta = DL[k][:1, :]
            qn = QA[k][:, :BLK]
            dq = None
            for c in range(NCHUNK):
                if c < 4:
                    v = HX[j, chunks[c], :]
                else:
                    v = T3[j, 1, (c - 4) * KC : (c - 3) * KC, :]
                p = PB[k][c]
                dp = dot_nn(v, dts)
                ds = (p.astype(f32) * (dp - delta)).astype(bf16)
                DV[chunks[c], :] += dot_nt(p, dts)
                yield
                DK[chunks[c], :] += dot_nn(ds, qn)
                term = dot_nn(KT[:, chunks[c]], ds)
                dq = term if dq is None else dq + term
                yield
            DQ[span(q0, QT, QT), :] = dq.T

        tiles = OWN // QT
        woven(forward(0, 0))

        def pair(v, _):
            woven(forward(2 * v + 1, 1), backward(2 * v, 0))
            woven(forward(2 * v + 2, 0), backward(2 * v + 1, 1))
            between(v)
            return 0

        lax.fori_loop(0, tiles // 2 - 1, pair, 0)
        woven(forward(tiles - 1, 1), backward(tiles - 2, 0))
        woven(backward(tiles - 1, 1))

        for d in ALL:
            cp_att(j, d).start()
        lo_att(j).start()

        for k in range(2):
            rows = slice(k * (OWN + SLAB), k * (OWN + SLAB) + SLAB)
            r = RB[rows, :]
            t = (gk * DK[rows, :]) * SCALE
            AH[j, k] = (DV[rows, :] + r * t).astype(bf16)
            MH[k] += (HX[j, rows, :].astype(f32) * r) * t
        for d in SIDES:
            cp_ah(j, d).start()
        TGP[j, 0] = (DK[EXT:, :] * SCALE).astype(bf16)
        TGP[j, 1] = DV[EXT:, :].astype(bf16)
        TG1[j, x] = TGP[j, :, block(x), :]
        for d in ALL:
            cp_rs(j, d).start()

        def own(i, _):
            rows = slab(i)
            qrows = oslab(i)
            r = RB[rows, :]
            t = (gq * DQ[qrows, :] + gk * DK[rows, :]) * SCALE
            AFS[par, qrows, :] = DV[rows, :] + r * t
            M[qrows, :] += (HX[j, rows, :].astype(f32) * r) * t
            return 0

        lax.fori_loop(0, NY, own, 0)

    def stage_d(j):
        par = lax.rem(j, 2)
        for d in SIDES:
            cp_ah(j, d, True).wait_recv()
        for i in range(NY):
            rows = slice(i * SLAB, (i + 1) * SLAB)
            a = AFS[par, rows, :]
            if i == 0:
                a = a + AHR[j, 0].astype(f32)
            if i == NY - 1:
                a = a + AHR[j, 1].astype(f32)
            AO[j, rows, :] = a.astype(bf16)
        for d in FOUR:
            cp_a(j, d).start()
        for d in ALL:
            cp_rs(j, d, True).wait_recv()
        for kv in range(2):
            total = TG1[j, 0, kv].astype(f32)
            for k in range(1, NX):
                total = total + TG1[j, k, kv].astype(f32)
            TG2[j, kv] = total.astype(bf16)
        TGY[j, :, block(y)] = TG2[j, 0]
        TGX[j, block(x), :] = TG2[j, 1]
        for d in ALL:
            cp_g1k(j, d).start()
            cp_g1v(j, d).start()

    def stage_e(j):
        for d in ALL:
            cp_g1k(j, d, True).wait_recv()
            cp_g1v(j, d, True).wait_recv()
        for d in ALL:
            cp_g2k(j, d).start()
            cp_g2v(j, d).start()
        lo_g2k(j).start()
        lo_g2v(j).start()

    barrier = pltpu.get_barrier_semaphore()
    for d in ALL:
        pl.semaphore_signal(barrier, inc=1, device_id=yid(d), device_id_type=MESH)
        pl.semaphore_signal(barrier, inc=1, device_id=xid(d), device_id_type=MESH)
    for d in FOUR:
        pl.semaphore_signal(barrier, inc=1, device_id=above(d), device_id_type=MESH)
    load = pltpu.make_async_copy(hid, HS, loc1.at[0])
    load.start()

    def first_local(j, _):
        lo_h(j).start()
        lo_tx(j).start()
        lo_do(j).start()
        return 0

    lax.fori_loop(0, STEPS, first_local, 0)
    pl.semaphore_wait(barrier, 10)

    front(0)
    cp_hu().start()

    lane = lax.broadcasted_iota(jnp.int32, (BLK, BLK), 1)

    def marks(b, _):
        KA[block(b), BLK:] = jnp.where(lane == b, 1.0, 0.0).astype(bf16)
        return 0

    lax.fori_loop(0, EXT // BLK, marks, 0)
    KA[EXT:, BLK:] = jnp.zeros((TXT, BLK), bf16)
    VT[BLK:, :] = jnp.ones((16, KEYS), bf16)

    def clear_m(i, _):
        M[oslab(i), :] = jnp.zeros((SLAB, BLK), f32)
        return 0

    lax.fori_loop(0, NY, clear_m, 0)
    for k in range(2):
        MH[k] = jnp.zeros((SLAB, BLK), f32)

    load.wait()

    for b in range(SLAB // BLK):
        h = HS[b * BLK : (b + 1) * BLK, :].astype(f32)
        mean = jnp.sum(h * h, axis=1, keepdims=True) * (1.0 / WIDTH)
        RT[8 * b : 8 * b + 8, :] = packed(lax.rsqrt(mean + EPS))[0]
    for d in ALL:
        cp_r(d).start()
    cp_ru().start()
    RTX[span(24 + 24 * y, 24, 8), :] = RT[...]
    for d in ALL:
        cp_r(d, True).wait_recv()
    for d in SIDES:
        cp_rh(d).start()
    for d in SIDES:
        cp_rh(d, True).wait_recv()
    stage_a(0)
    front(1)
    for b in range(EXT // BLK):
        RB[b * BLK : (b + 1) * BLK, :] = unpacked(RTX[8 * b : 8 * b + 8, :])
    stage_b(0)
    front(2)
    stage_a(1)

    def step(j, _):
        def between(v):
            @pl.when((v == 0) & (j + 1 < STEPS))
            def _():
                stage_b(j + 1)

            @pl.when((v == 1) & (j + 2 < STEPS))
            def _():
                stage_a(j + 2)

            @pl.when((v == 1) & (j + 3 < STEPS))
            def _():
                front(j + 3)

        stage_c(j, between)

        @pl.when(j >= 1)
        def _():
            stage_d(j - 1)

        @pl.when(j >= 2)
        def _():
            stage_e(j - 2)

        return 0

    lax.fori_loop(0, STEPS, step, 0)

    for k in range(2):
        tiles = packed(jnp.sum(MH[k], axis=1, keepdims=True))
        for b in range(SLAB // BLK):
            MHS[k, 8 * b : 8 * b + 8, :] = tiles[b]
    for d in SIDES:
        cp_mh(d).start()
    for b in range(OWN // BLK):
        column = jnp.sum(M[b * BLK : (b + 1) * BLK, :], axis=1, keepdims=True)
        MT[8 * b : 8 * b + 8, :] = packed(column)[0]
    stage_d(STEPS - 1)
    for d in SIDES:
        cp_mh(d, True).wait_recv()
    MT[:24, :] += MHR[0]
    MT[72:96, :] += MHR[1]
    for d in FOUR:
        cp_m(d).start()
    stage_e(STEPS - 2)
    cp_hu().wait_recv()
    cp_ru().wait_recv()
    for d in FOUR:
        cp_m(d, True).wait_recv()

    def arrived(j, _):
        for d in FOUR:
            cp_a(j, d, True).wait_recv()
        return 0

    lax.fori_loop(0, STEPS, arrived, 0)
    for b in range(SLAB // BLK):
        rows = slice(b * BLK, (b + 1) * BLK)
        tiles = slice(8 * b, 8 * b + 8)
        mean = (MR[0, tiles] + MR[1, tiles] + MR[2, tiles] + MR[3, tiles]) * (1.0 / WIDTH)
        r = RU[tiles, :]
        factor = unpacked(mean * (r * r))[:, :1]
        grad = AF[rows, :].astype(f32) - HU[rows, :].astype(f32) * factor
        DH[rows, :] = jnp.where(section < sections - 1, grad, 0.0).astype(bf16)
    store = pltpu.make_async_copy(DH, dh_out, loc1.at[1])
    store.start()
    stage_e(STEPS - 1)
    store.wait()

    def last(j, _):
        for d in ALL:
            cp_att(j, d, True).wait_recv()
            cp_g2k(j, d, True).wait_recv()
            cp_g2v(j, d, True).wait_recv()
            for copy in (cp_h, cp_do, cp_tx, cp_ty, cp_tg, cp_att, cp_rs, cp_g1k, cp_g1v, cp_g2k, cp_g2v):
                copy(j, d).wait_send()
        for d in FOUR:
            cp_a(j, d).wait_send()
        for d in SIDES:
            cp_halo(j, d).wait_send()
            cp_ah(j, d).wait_send()
        lo_att(j).wait()
        lo_g2k(j).wait()
        lo_g2v(j).wait()
        return 0

    lax.fori_loop(0, STEPS, last, 0)
    for d in ALL:
        cp_r(d).wait_send()
    for d in FOUR:
        cp_m(d).wait_send()
    cp_hu().wait_send()
    cp_ru().wait_send()
    for d in SIDES:
        cp_rh(d).wait_send()
        cp_mh(d).wait_send()


def query_bias(pattern, x):
    blocks = OWN // BLK
    reach = SLAB // BLK
    span_ = pattern.shape[1]
    rows = lax.dynamic_slice_in_dim(pattern, x * blocks, blocks, 0)
    first = jnp.arange(blocks, dtype=jnp.int32)[:, None]
    col = jnp.arange(BLK, dtype=jnp.int32)[None, :]
    offset = col - first
    picked = sum(jnp.where(offset == k, rows[:, k : k + 1], 0) for k in range(span_))
    globe = x * blocks - reach + col
    inside = (globe >= 0) & (globe < pattern.shape[0])
    allowed = ((picked > 0) & inside) | (col >= EXT // BLK)
    return jnp.where(allowed, 0.0, NEG).astype(f32)


def local(hidden, query_norm_gain, key_norm_gain, text_kv, holder, pattern, grad_out):
    x = lax.axis_index("seq") // NY
    qbias = query_bias(pattern, x)
    who = holder[0]
    row = lax.broadcasted_iota(jnp.int32, (NX + NY, NY * BLK), 0)
    select = jnp.where(row < NX, row == who // NY, row - NX == who % NY).astype(f32)
    heads = WIDTH // HDIM
    any_spec = pl.BlockSpec(memory_space=pl.ANY)
    vmem = pl.BlockSpec(memory_space=pltpu.VMEM)

    def V(*shape, dtype=bf16):
        return pltpu.VMEM(shape, dtype)

    attended, upstream, text_total = pl.pallas_call(
        kernel,
        out_shape=(
            jax.ShapeDtypeStruct((SLAB, WIDTH), bf16),
            jax.ShapeDtypeStruct((SLAB, WIDTH), bf16),
            jax.ShapeDtypeStruct((2, TXT, WIDTH), bf16),
        ),
        in_specs=[any_spec] * 3 + [vmem] * 4,
        out_specs=[any_spec] * 3,
        scratch_shapes=[
            V(SLAB, WIDTH),
            V(SLAB, WIDTH),
            V(24, BLK, dtype=f32),
            V(STEPS, EXT, BLK),
            V(STEPS, OWN, BLK),
            V(EXT // BLK * 8, BLK, dtype=f32),
            V(24, BLK, dtype=f32),
            V(EXT, BLK, dtype=f32),
            V(STEPS, NX, 2, BLK, NY * BLK),
            V(STEPS, 2, BLK, NY * BLK),
            V(STEPS, NY, 2, BLK, BLK),
            V(STEPS, 2, TXT, BLK),
            V(KEYS, 2 * BLK),
            V(BLK, KEYS),
            V(BLK + 16, KEYS),
            V(QT, 2 * BLK),
            V(QT, 2 * BLK),
            V(NCHUNK, KC, QT, dtype=f32),
            V(NCHUNK, KC, QT),
            V(NCHUNK, KC, QT),
            V(BLK, QT),
            V(BLK, QT),
            V(8, QT, dtype=f32),
            V(8, QT, dtype=f32),
            V(KEYS, BLK, dtype=f32),
            V(KEYS, BLK, dtype=f32),
            V(OWN, BLK, dtype=f32),
            V(STEPS, OWN, BLK),
            V(2, OWN, BLK, dtype=f32),
            V(STEPS, 2, SLAB, BLK),
            V(STEPS, 2, SLAB, BLK),
            V(STEPS, OWN, BLK),
            V(SLAB, WIDTH),
            V(OWN, BLK, dtype=f32),
            V(2, SLAB, BLK, dtype=f32),
            V(96, BLK, dtype=f32),
            V(2, 24, BLK, dtype=f32),
            V(2, 24, BLK, dtype=f32),
            V(NY, 24, BLK, dtype=f32),
            V(STEPS, 2, TXT, BLK),
            V(STEPS, NX, 2, BLK, BLK),
            V(STEPS, 2, BLK, BLK),
            V(STEPS, BLK, NY * BLK),
            V(STEPS, TXT, BLK),
            V(SLAB, WIDTH),
            pltpu.SemaphoreType.DMA((KINDS, STEPS, 8)),
            pltpu.SemaphoreType.DMA((KINDS, STEPS, 8)),
            pltpu.SemaphoreType.DMA((5, 4)),
            pltpu.SemaphoreType.DMA((5, 4)),
            pltpu.SemaphoreType.DMA((6, STEPS)),
            pltpu.SemaphoreType.DMA((2,)),
        ],
        compiler_params=pltpu.CompilerParams(
            collective_id=0, has_side_effects=True, vmem_limit_bytes=60 * 1024 * 1024
        ),
        cost_estimate=pl.CostEstimate(
            flops=24 * 10**9, bytes_accessed=40 * 10**6, transcendentals=12 * 10**6
        ),
        name="attention",
    )(
        hidden[0],
        grad_out[0],
        text_kv[0, 0],
        query_norm_gain.reshape(heads, HDIM),
        key_norm_gain.reshape(heads, HDIM),
        select,
        qbias,
    )
    return (attended[None], upstream[None], text_total[None])


def solution(mesh):
    in_specs = (
        P("section", "seq", None),
        P("section", None),
        P("section", None),
        P("section", "seq", None, None, None),
        P("section"),
        P(),
        P("section", "seq", None),
    )
    out_specs = (
        P("section", "seq", None),
        P("section", "seq", None),
        P("section", None, None, None),
    )
    return jax.shard_map(local, mesh=mesh, in_specs=in_specs, out_specs=out_specs, check_vma=False)
```

```python
import jax
import jax.numpy as jnp
from jax import lax
from jax.experimental import pallas as pl
from jax.experimental.pallas import tpu as pltpu
from jax.sharding import PartitionSpec as P

HDIM = 128
BLK = 128
EPS = 1e-06
MESH = pl.DeviceIdType.MESH

NX = 4
NY = 4
SLAB = 384
TXT = 512
WIDTH = 2560
STEPS = 5
OWN = NY * SLAB
EXT = OWN + 2 * SLAB
KEYS = EXT + TXT
QT = 256
KC = 256
NCHUNK = 4 + TXT // KC
SCALE = HDIM ** (-0.5)
LOG2E = 1.4426950408889634
NEG = -1e30

(
    K_H,
    K_DO,
    K_TX,
    K_TY,
    K_TG,
    K_HALO,
    K_ATT,
    K_AH,
    K_A,
    K_RS,
    K_G1,
    K_G2,
    K_G3,
) = range(13)
KINDS = 13
O_R, O_RH, O_MH, O_M, O_HU = range(5)

f32 = jnp.float32
bf16 = jnp.bfloat16


def dot_nn(a, b):
    return lax.dot_general(a, b, (((1,), (0,)), ((), ())), preferred_element_type=f32)


def dot_nt(a, b):
    return lax.dot_general(a, b, (((1,), (1,)), ((), ())), preferred_element_type=f32)


def woven(*parts):
    parts = list(parts)
    while parts:
        for part in list(parts):
            if next(part, True):
                parts.remove(part)


def block(k):
    return pl.ds(pl.multiple_of(k * BLK, BLK), BLK)


def span(start, size, unit):
    return pl.ds(pl.multiple_of(start, unit), size)


def packed(column):
    rows = column.shape[0]
    wide = jnp.broadcast_to(column, (rows, BLK))
    return [wide[b * BLK : (b + 1) * BLK].T[:8] for b in range(rows // BLK)]


def unpacked(tile):
    return jnp.broadcast_to(tile[:1], (BLK, BLK)).T


def kernel(
    hid, do_in, txt, gq_ref, gk_ref, sel_ref, qb_ref,
    att_out, dh_out, tg_out,
    HS, HU, RU, HX, DO, RTX, RT, RB, TP, TQ, TM, T1, TS, T2, T3, KA, KT, VT, QA0, QA1, S, PB0, PB1, DTS0, DTS1, DL0, DL1, DK, DV, DQ,
    ATT, AFS, AH, AHR, AO, AF, M, MH, MT, MHS, MHR, MR, TGP, TG1, TG2, TGY, TGX, DH,
    send, recv, once_send, once_recv, loc, loc1,
):
    QA, PB, DTS, DL = (QA0, QA1), (PB0, PB1), (DTS0, DTS1), (DL0, DL1)
    seq = lax.axis_index("seq")
    section = lax.axis_index("section")
    sections = lax.axis_size("section")
    x = lax.div(seq, NY)
    y = lax.rem(seq, NY)

    def ry(d):
        return lax.rem(y + (d + NY), NY)

    def rx(d):
        return lax.rem(x + (d + NX), NX)

    def yid(d):
        return {"seq": x * NY + ry(d)}

    def xid(d):
        return {"seq": rx(d) * NY + y}

    def below(d):
        return {"seq": x * NY + ry(d), "section": lax.rem(section + (sections - 1), sections)}

    def above(d):
        return {"seq": x * NY + ry(d), "section": lax.rem(section + 1, sections)}

    def rc(src, dst, kind, j, d, dev):
        return pltpu.make_async_remote_copy(
            src_ref=src, dst_ref=dst, send_sem=send.at[kind, j, d],
            recv_sem=recv.at[kind, j, d], device_id=dev, device_id_type=MESH,
        )

    def rc1(src, dst, kind, d, dev):
        return pltpu.make_async_remote_copy(
            src_ref=src, dst_ref=dst, send_sem=once_send.at[kind, d],
            recv_sem=once_recv.at[kind, d], device_id=dev, device_id_type=MESH,
        )

    def hcol(j, yy):
        return block(NY * j + yy)

    def wide(j):
        return span(j * (NY * BLK), NY * BLK, NY * BLK)

    def slab(yy):
        return span(SLAB + SLAB * yy, SLAB, SLAB)

    def oslab(yy):
        return span(SLAB * yy, SLAB, SLAB)

    def cp_h(j, d, w=False):
        return rc(hid.at[:, hcol(j, ry(d))], HX.at[j, slab(ry(-d) if w else y), :], K_H, j, d, yid(d))

    def cp_do(j, d, w=False):
        return rc(do_in.at[:, hcol(j, ry(d))], DO.at[j, oslab(ry(-d) if w else y), :], K_DO, j, d, yid(d))

    def cp_tx_far(j, d, w=False):
        kv = 0 if d == 1 else 1
        return rc(txt.at[kv, block(rx(2)), wide(j)], TP.at[j, kv], K_TX, j, d, xid(d))

    def cp_tx_near(j, d, w=False):
        side, kv = (0, 1) if d == 1 else (1, 0)
        return rc(txt.at[kv, block(rx(d)), wide(j)], T1.at[j, side, kv], K_TX, j, 4 + d, xid(d))

    def cp_tx_pass(j, d, w=False):
        kv = 0 if d == 1 else 1
        return rc(TM.at[j, kv], T1.at[j, kv, kv], K_TX, j, 1 + d, xid(d))

    def cp_ty(j, d, w=False):
        return rc(TS.at[j, :, :, block(ry(d))], T2.at[j, ry(-d) if w else y], K_TY, j, d, yid(d))

    def cp_tg(j, d, w=False):
        return rc(T3.at[j, :, block(x), :], T3.at[j, :, block(rx(-d) if w else x), :], K_TG, j, d, xid(d))

    def cp_halo(j, d, w=False):
        if d == 1:
            return rc(HX.at[j, pl.ds(OWN, SLAB), :], HX.at[j, pl.ds(0, SLAB), :], K_HALO, j, 1, xid(1))
        return rc(HX.at[j, pl.ds(SLAB, SLAB), :], HX.at[j, pl.ds(OWN + SLAB, SLAB), :], K_HALO, j, 3, xid(3))

    def cp_att(j, d, w=False):
        return rc(ATT.at[j, oslab(ry(d)), :], att_out.at[:, hcol(j, ry(-d) if w else y)], K_ATT, j, d, yid(d))

    def cp_ah(j, d, w=False):
        k = 1 if d == 1 else 0
        return rc(AH.at[j, k], AHR.at[j, 1 - k], K_AH, j, d, xid(d))

    def cp_a(j, d, w=False):
        return rc(AO.at[j, oslab(ry(d)), :], AF.at[:, hcol(j, ry(-d) if w else y)], K_A, j, d, below(d))

    def cp_rs(j, d, w=False):
        return rc(TGP.at[j, :, block(rx(d)), :], TG1.at[j, rx(-d) if w else x], K_RS, j, d, xid(d))

    def cp_g1k(j, d, w=False):
        return rc(TG2.at[j, 0], TGY.at[j, :, block(ry(-d) if w else y)], K_G1, j, d, yid(d))

    def cp_g1v(j, d, w=False):
        return rc(TG2.at[j, 1], TGX.at[j, block(rx(-d) if w else x), :], K_G1, j, 4 + d, xid(d))

    def cp_g2k(j, d, w=False):
        return rc(TGY.at[j], tg_out.at[0, block(rx(-d) if w else x), wide(j)], K_G2, j, d, xid(d))

    def cp_g2v(j, d, w=False):
        return rc(TGX.at[j], tg_out.at[1, :, hcol(j, ry(-d) if w else y)], K_G2, j, 4 + d, yid(d))

    def cp_g3k(j, d, w=False):
        part = 0 if d == 1 else 1
        who = rx(2) if w else rx(-d)
        half = BLK // 2
        rows = span(who * BLK + part * half, half, half)
        return rc(tg_out.at[0, rows, wide(j)], tg_out.at[0, rows, wide(j)], K_G3, j, d, xid(d))

    def cp_g3v(j, d, w=False):
        part = 0 if d == 1 else 1
        who = ry(2) if w else ry(-d)
        rows = pl.ds(part * (TXT // 2), TXT // 2)
        return rc(tg_out.at[1, rows, hcol(j, who)], tg_out.at[1, rows, hcol(j, who)], K_G3, j, 4 + d, yid(d))

    def cp_r(d, w=False):
        return rc1(RT, RTX.at[span(24 + 24 * (ry(-d) if w else y), 24, 8), :], O_R, d, yid(d))

    def cp_rh(d, w=False):
        if d == 1:
            return rc1(RTX.at[pl.ds(96, 24), :], RTX.at[pl.ds(0, 24), :], O_RH, 1, xid(1))
        return rc1(RTX.at[pl.ds(24, 24), :], RTX.at[pl.ds(120, 24), :], O_RH, 3, xid(3))

    def cp_mh(d, w=False):
        k = 1 if d == 1 else 0
        return rc1(MHS.at[k], MHR.at[1 - k], O_MH, d, xid(d))

    def cp_m(d, w=False):
        return rc1(MT.at[span(24 * ry(d), 24, 8), :], MR.at[ry(-d) if w else y], O_M, d, below(d))

    def cp_hu():
        return rc1(hid, HU, O_HU, 0, below(0))

    def cp_ru():
        return rc1(RT, RU, O_HU, 1, below(0))

    def lo_h(j):
        return pltpu.make_async_copy(hid.at[:, hcol(j, y)], HX.at[j, slab(y), :], loc.at[0, j])

    def lo_do(j):
        return pltpu.make_async_copy(do_in.at[:, hcol(j, y)], DO.at[j, oslab(y), :], loc.at[1, j])

    def lo_tx(j):
        return pltpu.make_async_copy(txt.at[:, block(x), wide(j)], T1.at[j, 2], loc.at[2, j])

    def lo_pass(j, kv):
        where = rx(1) if kv == 0 else rx(-1)
        return pltpu.make_async_copy(txt.at[kv, block(where), wide(j)], TQ.at[j, kv], loc.at[6 + kv, j])

    def lo_att(j):
        return pltpu.make_async_copy(ATT.at[j, oslab(y), :], att_out.at[:, hcol(j, y)], loc.at[3, j])

    def lo_g2k(j):
        return pltpu.make_async_copy(TGY.at[j], tg_out.at[0, block(x), wide(j)], loc.at[4, j])

    def lo_g2v(j):
        return pltpu.make_async_copy(TGX.at[j], tg_out.at[1, :, hcol(j, y)], loc.at[5, j])

    ALL = (1, 3, 2)
    FOUR = (0, 1, 3, 2)
    SIDES = (1, 3)

    def front(j):
        for d in SIDES:
            cp_tx_far(j, d).start()
        for d in SIDES:
            cp_tx_near(j, d).start()
        for d in ALL:
            cp_h(j, d).start()
        for d in ALL:
            cp_do(j, d).start()

    def stage_p(j):
        for kv in range(2):
            lo_pass(j, kv).wait()
            cp_tx_far(j, 1 if kv == 0 else 3, True).wait_recv()
            far = sel_ref[3:4, :] if kv == 0 else sel_ref[1:2, :]
            part = TP[j, kv].astype(f32) * far + TQ[j, kv].astype(f32) * (1.0 - far)
            TM[j, kv] = part.astype(bf16)
            cp_tx_pass(j, 1 if kv == 0 else 3).start()

    def stage_a(j):
        lo_tx(j).wait()
        for d in SIDES:
            cp_tx_near(j, d, True).wait_recv()
            cp_tx_pass(j, d, True).wait_recv()
        here, up, two, down = (sel_ref[k : k + 1, :] for k in range(NX))
        for kv in range(2):
            low, high = (down + two, up) if kv == 0 else (down, up + two)
            part = T1[j, 2, kv].astype(f32) * here
            part = part + T1[j, 0, kv].astype(f32) * low
            part = part + T1[j, 1, kv].astype(f32) * high
            TS[j, kv] = part.astype(bf16)
        T2[j, y] = TS[j, :, :, block(y)]
        for d in ALL:
            cp_ty(j, d).start()
        lo_h(j).wait()
        for d in ALL:
            cp_h(j, d, True).wait_recv()
        for d in SIDES:
            cp_halo(j, d).start()

    def stage_b(j):
        for d in ALL:
            cp_ty(j, d, True).wait_recv()
        for kv in range(2):
            part = jnp.zeros((BLK, BLK), f32)
            for k in range(NY):
                part = part + T2[j, k, kv].astype(f32) * sel_ref[NX + k : NX + k + 1, :BLK]
            T3[j, kv, block(x), :] = part.astype(bf16)
        for d in ALL:
            cp_tg(j, d).start()

    def stage_c(j, between):
        for d in SIDES:
            cp_halo(j, d, True).wait_recv()
        lo_do(j).wait()
        for d in ALL:
            cp_do(j, d, True).wait_recv()
            cp_tg(j, d, True).wait_recv()
        head = NY * j + y
        gq = gq_ref[pl.ds(head, 1), :]
        gk = gk_ref[pl.ds(head, 1), :]
        par = lax.rem(j, 2)

        def prep(b, _):
            rows = block(b)
            h = HX[j, rows, :].astype(f32)
            kn = (h * RB[rows, :]) * gk
            KA[rows, :BLK] = kn.astype(bf16)
            KT[:, rows] = kn.astype(bf16).T
            VT[:BLK, rows] = HX[j, rows, :].T
            return 0

        lax.fori_loop(0, EXT // BLK, prep, 0)
        for b in range(TXT // BLK):
            rows = slice(EXT + b * BLK, EXT + (b + 1) * BLK)
            kn = T3[j, 0, b * BLK : (b + 1) * BLK, :]
            KA[rows, :BLK] = kn
            KT[:, rows] = kn.T
            VT[:BLK, rows] = T3[j, 1, b * BLK : (b + 1) * BLK, :].T

        def clear(b, _):
            rows = span(b * KC, KC, KC)
            DK[rows, :] = jnp.zeros((KC, BLK), f32)
            DV[rows, :] = jnp.zeros((KC, BLK), f32)
            return 0

        lax.fori_loop(0, KEYS // KC, clear, 0)

        def chunks_of(q0):
            chunks = [span(q0 + KC * c, KC, KC) for c in range(4)]
            return chunks + [pl.ds(EXT + KC * c, KC) for c in range(TXT // KC)]

        def forward(u, k):
            q0 = u * QT
            qrows = span(q0, QT, QT)
            erows = span(SLAB + q0, QT, BLK)
            h = HX[j, erows, :].astype(f32)
            QA[k][:, :BLK] = ((h * RB[erows, :]) * gq).astype(bf16)
            for b in range(QT // BLK):
                bias = qb_ref[pl.ds(u * (QT // BLK) + b, 1), :].astype(bf16)
                QA[k][b * BLK : (b + 1) * BLK, BLK:] = jnp.broadcast_to(bias, (BLK, BLK))
            qa = QA[k][...]
            chunks = chunks_of(q0)
            top = None
            for c in range(NCHUNK):
                s = dot_nt(KA[chunks[c], :], qa)
                S[c] = s
                high = jnp.max(s, axis=0, keepdims=True)
                top = high if top is None else jnp.maximum(top, high)
                yield
            top = top * (SCALE * LOG2E)
            dt = DO[j, qrows, :].astype(f32).T
            ot = None
            for c in range(NCHUNK):
                p = jnp.exp2(S[c] * (SCALE * LOG2E) - top).astype(bf16)
                PB[k][c] = p
                term = dot_nn(VT[:, chunks[c]], p)
                ot = term if ot is None else ot + term
                yield
            inv = 1.0 / ot[BLK : BLK + 1, :]
            o = ot[:BLK, :] * inv
            delta = jnp.sum(dt * o, axis=0, keepdims=True) * inv
            DTS[k][...] = (dt * inv).astype(bf16)
            DL[k][...] = jnp.broadcast_to(delta, (8, QT))
            ATT[j, qrows, :] = o.T.astype(bf16)

        def backward(u, k):
            q0 = u * QT
            chunks = chunks_of(q0)
            dts = DTS[k][...]
            delta = DL[k][:1, :]
            qn = QA[k][:, :BLK]
            dq = None
            for c in range(NCHUNK):
                if c < 4:
                    v = HX[j, chunks[c], :]
                else:
                    v = T3[j, 1, (c - 4) * KC : (c - 3) * KC, :]
                p = PB[k][c]
                dp = dot_nn(v, dts)
                ds = (p.astype(f32) * (dp - delta)).astype(bf16)
                DV[chunks[c], :] += dot_nt(p, dts)
                yield
                DK[chunks[c], :] += dot_nn(ds, qn)
                term = dot_nn(KT[:, chunks[c]], ds)
                dq = term if dq is None else dq + term
                yield
            DQ[span(q0, QT, QT), :] = dq.T

        tiles = OWN // QT
        woven(forward(0, 0))

        def pair(v, _):
            woven(forward(2 * v + 1, 1), backward(2 * v, 0))
            woven(forward(2 * v + 2, 0), backward(2 * v + 1, 1))
            between(v)
            return 0

        lax.fori_loop(0, tiles // 2 - 1, pair, 0)
        woven(forward(tiles - 1, 1), backward(tiles - 2, 0))
        woven(backward(tiles - 1, 1))

        for d in ALL:
            cp_att(j, d).start()
        lo_att(j).start()

        for k in range(2):
            rows = slice(k * (OWN + SLAB), k * (OWN + SLAB) + SLAB)
            r = RB[rows, :]
            t = (gk * DK[rows, :]) * SCALE
            AH[j, k] = (DV[rows, :] + r * t).astype(bf16)
            MH[k] += (HX[j, rows, :].astype(f32) * r) * t
        for d in SIDES:
            cp_ah(j, d).start()
        TGP[j, 0] = (DK[EXT:, :] * SCALE).astype(bf16)
        TGP[j, 1] = DV[EXT:, :].astype(bf16)
        TG1[j, x] = TGP[j, :, block(x), :]
        for d in ALL:
            cp_rs(j, d).start()

        def own(i, _):
            rows = slab(i)
            qrows = oslab(i)
            r = RB[rows, :]
            t = (gq * DQ[qrows, :] + gk * DK[rows, :]) * SCALE
            AFS[par, qrows, :] = DV[rows, :] + r * t
            M[qrows, :] += (HX[j, rows, :].astype(f32) * r) * t
            return 0

        lax.fori_loop(0, NY, own, 0)

    def stage_d(j):
        par = lax.rem(j, 2)
        for d in SIDES:
            cp_ah(j, d, True).wait_recv()
        for i in range(NY):
            rows = slice(i * SLAB, (i + 1) * SLAB)
            a = AFS[par, rows, :]
            if i == 0:
                a = a + AHR[j, 0].astype(f32)
            if i == NY - 1:
                a = a + AHR[j, 1].astype(f32)
            AO[j, rows, :] = a.astype(bf16)
        for d in FOUR:
            cp_a(j, d).start()
        for d in ALL:
            cp_rs(j, d, True).wait_recv()
        for kv in range(2):
            total = TG1[j, 0, kv].astype(f32)
            for k in range(1, NX):
                total = total + TG1[j, k, kv].astype(f32)
            TG2[j, kv] = total.astype(bf16)
        TGY[j, :, block(y)] = TG2[j, 0]
        TGX[j, block(x), :] = TG2[j, 1]
        for d in ALL:
            cp_g1k(j, d).start()
            cp_g1v(j, d).start()

    def stage_e(j):
        for d in ALL:
            cp_g1k(j, d, True).wait_recv()
            cp_g1v(j, d, True).wait_recv()
        for d in SIDES:
            cp_g2k(j, d).start()
            cp_g2v(j, d).start()
        lo_g2k(j).start()
        lo_g2v(j).start()

    def stage_f(j):
        for d in SIDES:
            cp_g2k(j, d, True).wait_recv()
            cp_g3k(j, d).start()
            cp_g2v(j, d, True).wait_recv()
            cp_g3v(j, d).start()

    barrier = pltpu.get_barrier_semaphore()
    for d in ALL:
        pl.semaphore_signal(barrier, inc=1, device_id=yid(d), device_id_type=MESH)
        pl.semaphore_signal(barrier, inc=1, device_id=xid(d), device_id_type=MESH)
    for d in FOUR:
        pl.semaphore_signal(barrier, inc=1, device_id=above(d), device_id_type=MESH)
    load = pltpu.make_async_copy(hid, HS, loc1.at[0])
    load.start()

    def first_local(j, _):
        lo_h(j).start()
        lo_tx(j).start()
        lo_pass(j, 0).start()
        lo_pass(j, 1).start()
        lo_do(j).start()
        return 0

    lax.fori_loop(0, STEPS, first_local, 0)
    pl.semaphore_wait(barrier, 10)

    front(0)
    cp_hu().start()
    stage_p(0)

    lane = lax.broadcasted_iota(jnp.int32, (BLK, BLK), 1)

    def marks(b, _):
        KA[block(b), BLK:] = jnp.where(lane == b, 1.0, 0.0).astype(bf16)
        return 0

    lax.fori_loop(0, EXT // BLK, marks, 0)
    KA[EXT:, BLK:] = jnp.zeros((TXT, BLK), bf16)
    VT[BLK:, :] = jnp.ones((16, KEYS), bf16)

    def clear_m(i, _):
        M[oslab(i), :] = jnp.zeros((SLAB, BLK), f32)
        return 0

    lax.fori_loop(0, NY, clear_m, 0)
    for k in range(2):
        MH[k] = jnp.zeros((SLAB, BLK), f32)

    load.wait()

    for b in range(SLAB // BLK):
        h = HS[b * BLK : (b + 1) * BLK, :].astype(f32)
        mean = jnp.sum(h * h, axis=1, keepdims=True) * (1.0 / WIDTH)
        RT[8 * b : 8 * b + 8, :] = packed(lax.rsqrt(mean + EPS))[0]
    for d in ALL:
        cp_r(d).start()
    cp_ru().start()
    RTX[span(24 + 24 * y, 24, 8), :] = RT[...]
    for d in ALL:
        cp_r(d, True).wait_recv()
    for d in SIDES:
        cp_rh(d).start()
    for d in SIDES:
        cp_rh(d, True).wait_recv()
    stage_a(0)
    front(1)
    for b in range(EXT // BLK):
        RB[b * BLK : (b + 1) * BLK, :] = unpacked(RTX[8 * b : 8 * b + 8, :])
    stage_b(0)
    stage_p(1)
    front(2)
    stage_a(1)

    def step(j, _):
        def between(v):
            @pl.when((v == 0) & (j + 1 < STEPS))
            def _():
                stage_b(j + 1)

            @pl.when((v == 0) & (j + 2 < STEPS))
            def _():
                stage_p(j + 2)

            @pl.when((v == 1) & (j + 2 < STEPS))
            def _():
                stage_a(j + 2)

            @pl.when((v == 1) & (j + 3 < STEPS))
            def _():
                front(j + 3)

        stage_c(j, between)

        @pl.when(j >= 1)
        def _():
            stage_d(j - 1)

        @pl.when(j >= 2)
        def _():
            stage_e(j - 2)

        @pl.when(j >= 3)
        def _():
            stage_f(j - 3)

        return 0

    lax.fori_loop(0, STEPS, step, 0)

    for k in range(2):
        tiles = packed(jnp.sum(MH[k], axis=1, keepdims=True))
        for b in range(SLAB // BLK):
            MHS[k, 8 * b : 8 * b + 8, :] = tiles[b]
    for d in SIDES:
        cp_mh(d).start()
    stage_d(STEPS - 1)
    stage_e(STEPS - 2)
    for b in range(OWN // BLK):
        column = jnp.sum(M[b * BLK : (b + 1) * BLK, :], axis=1, keepdims=True)
        MT[8 * b : 8 * b + 8, :] = packed(column)[0]
    for d in SIDES:
        cp_mh(d, True).wait_recv()
    MT[:24, :] += MHR[0]
    MT[72:96, :] += MHR[1]
    for d in FOUR:
        cp_m(d).start()
    stage_e(STEPS - 1)
    stage_f(STEPS - 3)
    stage_f(STEPS - 2)
    cp_hu().wait_recv()
    cp_ru().wait_recv()
    for d in FOUR:
        cp_m(d, True).wait_recv()

    def arrived(j, _):
        for d in FOUR:
            cp_a(j, d, True).wait_recv()
        return 0

    lax.fori_loop(0, STEPS, arrived, 0)
    for b in range(SLAB // BLK):
        rows = slice(b * BLK, (b + 1) * BLK)
        tiles = slice(8 * b, 8 * b + 8)
        mean = (MR[0, tiles] + MR[1, tiles] + MR[2, tiles] + MR[3, tiles]) * (1.0 / WIDTH)
        r = RU[tiles, :]
        factor = unpacked(mean * (r * r))[:, :1]
        grad = AF[rows, :].astype(f32) - HU[rows, :].astype(f32) * factor
        DH[rows, :] = jnp.where(section < sections - 1, grad, 0.0).astype(bf16)
    store = pltpu.make_async_copy(DH, dh_out, loc1.at[1])
    store.start()
    stage_f(STEPS - 1)
    store.wait()

    def last(j, _):
        for d in ALL:
            cp_att(j, d, True).wait_recv()
            for copy in (cp_h, cp_do, cp_ty, cp_tg, cp_att, cp_rs, cp_g1k, cp_g1v):
                copy(j, d).wait_send()
        for d in FOUR:
            cp_a(j, d).wait_send()
        for d in SIDES:
            cp_g3k(j, d, True).wait_recv()
            cp_g3v(j, d, True).wait_recv()
            for copy in (cp_g2k, cp_g2v, cp_g3k, cp_g3v):
                copy(j, d).wait_send()
            cp_tx_far(j, d).wait_send()
            cp_tx_near(j, d).wait_send()
            cp_tx_pass(j, d).wait_send()
            cp_halo(j, d).wait_send()
            cp_ah(j, d).wait_send()
        lo_att(j).wait()
        lo_g2k(j).wait()
        lo_g2v(j).wait()
        return 0

    lax.fori_loop(0, STEPS, last, 0)
    for d in ALL:
        cp_r(d).wait_send()
    for d in FOUR:
        cp_m(d).wait_send()
    cp_hu().wait_send()
    cp_ru().wait_send()
    for d in SIDES:
        cp_rh(d).wait_send()
        cp_mh(d).wait_send()


def query_bias(pattern, x):
    blocks = OWN // BLK
    reach = SLAB // BLK
    span_ = pattern.shape[1]
    rows = lax.dynamic_slice_in_dim(pattern, x * blocks, blocks, 0)
    first = jnp.arange(blocks, dtype=jnp.int32)[:, None]
    col = jnp.arange(BLK, dtype=jnp.int32)[None, :]
    offset = col - first
    picked = sum(jnp.where(offset == k, rows[:, k : k + 1], 0) for k in range(span_))
    globe = x * blocks - reach + col
    inside = (globe >= 0) & (globe < pattern.shape[0])
    allowed = ((picked > 0) & inside) | (col >= EXT // BLK)
    return jnp.where(allowed, 0.0, NEG).astype(f32)


def local(hidden, query_norm_gain, key_norm_gain, text_kv, holder, pattern, grad_out):
    x = lax.axis_index("seq") // NY
    qbias = query_bias(pattern, x)
    who = holder[0]
    row = lax.broadcasted_iota(jnp.int32, (NX + NY, NY * BLK), 0)
    select = jnp.where(row < NX, row == (who // NY - x + NX) % NX, row - NX == who % NY).astype(f32)
    heads = WIDTH // HDIM
    any_spec = pl.BlockSpec(memory_space=pl.ANY)
    vmem = pl.BlockSpec(memory_space=pltpu.VMEM)

    def V(*shape, dtype=bf16):
        return pltpu.VMEM(shape, dtype)

    attended, upstream, text_total = pl.pallas_call(
        kernel,
        out_shape=(
            jax.ShapeDtypeStruct((SLAB, WIDTH), bf16),
            jax.ShapeDtypeStruct((SLAB, WIDTH), bf16),
            jax.ShapeDtypeStruct((2, TXT, WIDTH), bf16),
        ),
        in_specs=[any_spec] * 3 + [vmem] * 4,
        out_specs=[any_spec] * 3,
        scratch_shapes=[
            V(SLAB, WIDTH),
            V(SLAB, WIDTH),
            V(24, BLK, dtype=f32),
            V(STEPS, EXT, BLK),
            V(STEPS, OWN, BLK),
            V(EXT // BLK * 8, BLK, dtype=f32),
            V(24, BLK, dtype=f32),
            V(EXT, BLK, dtype=f32),
            V(STEPS, 2, BLK, NY * BLK),
            V(STEPS, 2, BLK, NY * BLK),
            V(STEPS, 2, BLK, NY * BLK),
            V(STEPS, 3, 2, BLK, NY * BLK),
            V(STEPS, 2, BLK, NY * BLK),
            V(STEPS, NY, 2, BLK, BLK),
            V(STEPS, 2, TXT, BLK),
            V(KEYS, 2 * BLK),
            V(BLK, KEYS),
            V(BLK + 16, KEYS),
            V(QT, 2 * BLK),
            V(QT, 2 * BLK),
            V(NCHUNK, KC, QT, dtype=f32),
            V(NCHUNK, KC, QT),
            V(NCHUNK, KC, QT),
            V(BLK, QT),
            V(BLK, QT),
            V(8, QT, dtype=f32),
            V(8, QT, dtype=f32),
            V(KEYS, BLK, dtype=f32),
            V(KEYS, BLK, dtype=f32),
            V(OWN, BLK, dtype=f32),
            V(STEPS, OWN, BLK),
            V(2, OWN, BLK, dtype=f32),
            V(STEPS, 2, SLAB, BLK),
            V(STEPS, 2, SLAB, BLK),
            V(STEPS, OWN, BLK),
            V(SLAB, WIDTH),
            V(OWN, BLK, dtype=f32),
            V(2, SLAB, BLK, dtype=f32),
            V(96, BLK, dtype=f32),
            V(2, 24, BLK, dtype=f32),
            V(2, 24, BLK, dtype=f32),
            V(NY, 24, BLK, dtype=f32),
            V(STEPS, 2, TXT, BLK),
            V(STEPS, NX, 2, BLK, BLK),
            V(STEPS, 2, BLK, BLK),
            V(STEPS, BLK, NY * BLK),
            V(STEPS, TXT, BLK),
            V(SLAB, WIDTH),
            pltpu.SemaphoreType.DMA((KINDS, STEPS, 8)),
            pltpu.SemaphoreType.DMA((KINDS, STEPS, 8)),
            pltpu.SemaphoreType.DMA((5, 4)),
            pltpu.SemaphoreType.DMA((5, 4)),
            pltpu.SemaphoreType.DMA((8, STEPS)),
            pltpu.SemaphoreType.DMA((2,)),
        ],
        compiler_params=pltpu.CompilerParams(
            collective_id=0, has_side_effects=True, vmem_limit_bytes=60 * 1024 * 1024
        ),
        cost_estimate=pl.CostEstimate(
            flops=24 * 10**9, bytes_accessed=40 * 10**6, transcendentals=12 * 10**6
        ),
        name="attention",
    )(
        hidden[0],
        grad_out[0],
        text_kv[0, 0],
        query_norm_gain.reshape(heads, HDIM),
        key_norm_gain.reshape(heads, HDIM),
        select,
        qbias,
    )
    return (attended[None], upstream[None], text_total[None])


def solution(mesh):
    in_specs = (
        P("section", "seq", None),
        P("section", None),
        P("section", None),
        P("section", "seq", None, None, None),
        P("section"),
        P(),
        P("section", "seq", None),
    )
    out_specs = (
        P("section", "seq", None),
        P("section", "seq", None),
        P("section", None, None, None),
    )
    return jax.shard_map(local, mesh=mesh, in_specs=in_specs, out_specs=out_specs, check_vma=False)
```

```python
import jax
import jax.numpy as jnp
from jax import lax
from jax.experimental import pallas as pl
from jax.experimental.pallas import tpu as pltpu
from jax.sharding import PartitionSpec as P

HDIM = 128
BLK = 128
EPS = 1e-06
MESH = pl.DeviceIdType.MESH

NX = 4
NY = 4
SLAB = 384
TXT = 512
WIDTH = 2560
STEPS = 5
OWN = NY * SLAB
EXT = OWN + 2 * SLAB
KEYS = EXT + TXT
QT = 256
KC = 256
NCHUNK = 4 + TXT // KC
SCALE = HDIM ** (-0.5)
LOG2E = 1.4426950408889634
NEG = -1e30

(
    K_H,
    K_DO,
    K_TX,
    K_TY,
    K_TG,
    K_HALO,
    K_ATT,
    K_AH,
    K_A,
    K_RS,
    K_G1,
    K_G2,
    K_G3,
) = range(13)
KINDS = 13
O_R, O_RH, O_MH, O_M, O_HU = range(5)

f32 = jnp.float32
bf16 = jnp.bfloat16


def dot_nn(a, b):
    return lax.dot_general(a, b, (((1,), (0,)), ((), ())), preferred_element_type=f32)


def dot_nt(a, b):
    return lax.dot_general(a, b, (((1,), (1,)), ((), ())), preferred_element_type=f32)


def woven(*parts):
    parts = list(parts)
    while parts:
        for part in list(parts):
            if next(part, True):
                parts.remove(part)


def block(k):
    return pl.ds(pl.multiple_of(k * BLK, BLK), BLK)


def span(start, size, unit):
    return pl.ds(pl.multiple_of(start, unit), size)


def packed(column):
    rows = column.shape[0]
    wide = jnp.broadcast_to(column, (rows, BLK))
    return [wide[b * BLK : (b + 1) * BLK].T[:8] for b in range(rows // BLK)]


def unpacked(tile):
    return jnp.broadcast_to(tile[:1], (BLK, BLK)).T


def kernel(
    hid, do_in, txt, gq_ref, gk_ref, sel_ref, qb_ref,
    att_out, dh_out, tg_out,
    HS, HU, RU, HX, DO, RTX, RT, RB, TP, TQ, TM, T1, TS, T2, T3, KA, KT, VT, QA0, QA1, S, PB0, PB1, DTS0, DTS1, DL0, DL1, DK, DV, DQ,
    ATT, AFS, AH, AHR, AO, AF, M, MH, MT, MHS, MHR, MR, TGP, TG1, TG2, TGY, TGX, DH,
    send, recv, once_send, once_recv, loc, loc1,
):
    QA, PB, DTS, DL = (QA0, QA1), (PB0, PB1), (DTS0, DTS1), (DL0, DL1)
    seq = lax.axis_index("seq")
    section = lax.axis_index("section")
    sections = lax.axis_size("section")
    x = lax.div(seq, NY)
    y = lax.rem(seq, NY)

    def ry(d):
        return lax.rem(y + (d + NY), NY)

    def rx(d):
        return lax.rem(x + (d + NX), NX)

    def yid(d):
        return {"seq": x * NY + ry(d)}

    def xid(d):
        return {"seq": rx(d) * NY + y}

    def below(d):
        return {"seq": x * NY + ry(d), "section": lax.rem(section + (sections - 1), sections)}

    def above(d):
        return {"seq": x * NY + ry(d), "section": lax.rem(section + 1, sections)}

    def rc(src, dst, kind, j, d, dev):
        return pltpu.make_async_remote_copy(
            src_ref=src, dst_ref=dst, send_sem=send.at[kind, j, d],
            recv_sem=recv.at[kind, j, d], device_id=dev, device_id_type=MESH,
        )

    def rc1(src, dst, kind, d, dev):
        return pltpu.make_async_remote_copy(
            src_ref=src, dst_ref=dst, send_sem=once_send.at[kind, d],
            recv_sem=once_recv.at[kind, d], device_id=dev, device_id_type=MESH,
        )

    def hcol(j, yy):
        return block(NY * j + yy)

    def wide(j):
        return span(j * (NY * BLK), NY * BLK, NY * BLK)

    def slab(yy):
        return span(SLAB + SLAB * yy, SLAB, SLAB)

    def oslab(yy):
        return span(SLAB * yy, SLAB, SLAB)

    def cp_h(j, d, w=False):
        return rc(hid.at[:, hcol(j, ry(d))], HX.at[j, slab(ry(-d) if w else y), :], K_H, j, d, yid(d))

    def cp_do(j, d, w=False):
        return rc(do_in.at[:, hcol(j, ry(d))], DO.at[j, oslab(ry(-d) if w else y), :], K_DO, j, d, yid(d))

    def cp_tx_far(j, d, w=False):
        kv = 0 if d == 1 else 1
        return rc(txt.at[kv, block(rx(2)), wide(j)], TP.at[j, kv], K_TX, j, d, xid(d))

    def cp_tx_near(j, d, w=False):
        side, kv = (0, 1) if d == 1 else (1, 0)
        return rc(txt.at[kv, block(rx(d)), wide(j)], T1.at[j, side, kv], K_TX, j, 4 + d, xid(d))

    def cp_tx_pass(j, d, w=False):
        kv = 0 if d == 1 else 1
        return rc(TM.at[j, kv], T1.at[j, kv, kv], K_TX, j, 1 + d, xid(d))

    def cp_ty(j, d, w=False):
        return rc(TS.at[j, :, :, block(ry(d))], T2.at[j, ry(-d) if w else y], K_TY, j, d, yid(d))

    def cp_tg(j, d, w=False):
        return rc(T3.at[j, :, block(x), :], T3.at[j, :, block(rx(-d) if w else x), :], K_TG, j, d, xid(d))

    def cp_halo(j, d, w=False):
        if d == 1:
            return rc(HX.at[j, pl.ds(OWN, SLAB), :], HX.at[j, pl.ds(0, SLAB), :], K_HALO, j, 1, xid(1))
        return rc(HX.at[j, pl.ds(SLAB, SLAB), :], HX.at[j, pl.ds(OWN + SLAB, SLAB), :], K_HALO, j, 3, xid(3))

    def cp_att(j, d, w=False):
        return rc(ATT.at[j, oslab(ry(d)), :], att_out.at[:, hcol(j, ry(-d) if w else y)], K_ATT, j, d, yid(d))

    def cp_ah(j, d, w=False):
        k = 1 if d == 1 else 0
        return rc(AH.at[j, k], AHR.at[j, 1 - k], K_AH, j, d, xid(d))

    def cp_a(j, d, w=False):
        return rc(AO.at[j, oslab(ry(d)), :], AF.at[:, hcol(j, ry(-d) if w else y)], K_A, j, d, below(d))

    def cp_rs(j, d, w=False):
        return rc(TGP.at[j, :, block(rx(d)), :], TG1.at[j, rx(-d) if w else x], K_RS, j, d, xid(d))

    def cp_g1k(j, d, w=False):
        return rc(TG2.at[j, 0], TGY.at[j, :, block(ry(-d) if w else y)], K_G1, j, d, yid(d))

    def cp_g1v(j, d, w=False):
        return rc(TG2.at[j, 1], TGX.at[j, block(rx(-d) if w else x), :], K_G1, j, 4 + d, xid(d))

    def cp_g2k(j, d, w=False):
        return rc(TGY.at[j], tg_out.at[0, block(rx(-d) if w else x), wide(j)], K_G2, j, d, xid(d))

    def cp_g2v(j, d, w=False):
        return rc(TGX.at[j], tg_out.at[1, :, hcol(j, ry(-d) if w else y)], K_G2, j, 4 + d, yid(d))

    def cp_g3k(j, d, w=False):
        part = 0 if d == 1 else 1
        who = rx(2) if w else rx(-d)
        half = BLK // 2
        rows = span(who * BLK + part * half, half, half)
        return rc(tg_out.at[0, rows, wide(j)], tg_out.at[0, rows, wide(j)], K_G3, j, d, xid(d))

    def cp_g3v(j, d, w=False):
        part = 0 if d == 1 else 1
        who = ry(2) if w else ry(-d)
        rows = pl.ds(part * (TXT // 2), TXT // 2)
        return rc(tg_out.at[1, rows, hcol(j, who)], tg_out.at[1, rows, hcol(j, who)], K_G3, j, 4 + d, yid(d))

    def cp_r(d, w=False):
        return rc1(RT, RTX.at[span(24 + 24 * (ry(-d) if w else y), 24, 8), :], O_R, d, yid(d))

    def cp_rh(d, w=False):
        if d == 1:
            return rc1(RTX.at[pl.ds(96, 24), :], RTX.at[pl.ds(0, 24), :], O_RH, 1, xid(1))
        return rc1(RTX.at[pl.ds(24, 24), :], RTX.at[pl.ds(120, 24), :], O_RH, 3, xid(3))

    def cp_mh(d, w=False):
        k = 1 if d == 1 else 0
        return rc1(MHS.at[k], MHR.at[1 - k], O_MH, d, xid(d))

    def cp_m(d, w=False):
        return rc1(MT.at[span(24 * ry(d), 24, 8), :], MR.at[ry(-d) if w else y], O_M, d, below(d))

    def cp_hu():
        return rc1(hid, HU, O_HU, 0, below(0))

    def cp_ru():
        return rc1(RT, RU, O_HU, 1, below(0))

    def lo_h(j):
        return pltpu.make_async_copy(hid.at[:, hcol(j, y)], HX.at[j, slab(y), :], loc.at[0, j])

    def lo_do(j):
        return pltpu.make_async_copy(do_in.at[:, hcol(j, y)], DO.at[j, oslab(y), :], loc.at[1, j])

    def lo_tx(j):
        return pltpu.make_async_copy(txt.at[:, block(x), wide(j)], T1.at[j, 2], loc.at[2, j])

    def lo_pass(j, kv):
        where = rx(1) if kv == 0 else rx(-1)
        return pltpu.make_async_copy(txt.at[kv, block(where), wide(j)], TQ.at[j, kv], loc.at[6 + kv, j])

    def lo_att(j):
        return pltpu.make_async_copy(ATT.at[j, oslab(y), :], att_out.at[:, hcol(j, y)], loc.at[3, j])

    def lo_g2k(j):
        return pltpu.make_async_copy(TGY.at[j], tg_out.at[0, block(x), wide(j)], loc.at[4, j])

    def lo_g2v(j):
        return pltpu.make_async_copy(TGX.at[j], tg_out.at[1, :, hcol(j, y)], loc.at[5, j])

    ALL = (1, 3, 2)
    FOUR = (0, 1, 3, 2)
    SIDES = (1, 3)

    def front(j):
        for d in SIDES:
            cp_tx_far(j, d).start()
        for d in SIDES:
            cp_tx_near(j, d).start()
        for d in ALL:
            cp_h(j, d).start()
        for d in ALL:
            cp_do(j, d).start()

    def stage_p(j):
        for kv in range(2):
            lo_pass(j, kv).wait()
            cp_tx_far(j, 1 if kv == 0 else 3, True).wait_recv()
            far = sel_ref[3:4, :] if kv == 0 else sel_ref[1:2, :]
            part = TP[j, kv].astype(f32) * far + TQ[j, kv].astype(f32) * (1.0 - far)
            TM[j, kv] = part.astype(bf16)
            cp_tx_pass(j, 1 if kv == 0 else 3).start()

    def stage_a(j):
        lo_tx(j).wait()
        for d in SIDES:
            cp_tx_near(j, d, True).wait_recv()
            cp_tx_pass(j, d, True).wait_recv()
        here, up, two, down = (sel_ref[k : k + 1, :] for k in range(NX))
        for kv in range(2):
            low, high = (down + two, up) if kv == 0 else (down, up + two)
            part = T1[j, 2, kv].astype(f32) * here
            part = part + T1[j, 0, kv].astype(f32) * low
            part = part + T1[j, 1, kv].astype(f32) * high
            TS[j, kv] = part.astype(bf16)
        T2[j, y] = TS[j, :, :, block(y)]
        for d in ALL:
            cp_ty(j, d).start()
        lo_h(j).wait()
        for d in ALL:
            cp_h(j, d, True).wait_recv()
        for d in SIDES:
            cp_halo(j, d).start()

    def stage_b(j):
        for d in ALL:
            cp_ty(j, d, True).wait_recv()
        for kv in range(2):
            part = jnp.zeros((BLK, BLK), f32)
            for k in range(NY):
                part = part + T2[j, k, kv].astype(f32) * sel_ref[NX + k : NX + k + 1, :BLK]
            T3[j, kv, block(x), :] = part.astype(bf16)
        for d in ALL:
            cp_tg(j, d).start()

    def stage_c(j, between):
        for d in SIDES:
            cp_halo(j, d, True).wait_recv()
        lo_do(j).wait()
        for d in ALL:
            cp_do(j, d, True).wait_recv()
            cp_tg(j, d, True).wait_recv()
        gq = gq_ref[:, hcol(j, y)]
        gk = gk_ref[:, hcol(j, y)]
        par = lax.rem(j, 2)

        def prep(b, _):
            rows = block(b)
            h = HX[j, rows, :].astype(f32)
            kn = (h * RB[rows, :]) * gk
            KA[rows, :BLK] = kn.astype(bf16)
            KT[:, rows] = kn.astype(bf16).T
            VT[:BLK, rows] = HX[j, rows, :].T
            return 0

        lax.fori_loop(0, EXT // BLK, prep, 0)
        for b in range(TXT // BLK):
            rows = slice(EXT + b * BLK, EXT + (b + 1) * BLK)
            kn = T3[j, 0, b * BLK : (b + 1) * BLK, :]
            KA[rows, :BLK] = kn
            KT[:, rows] = kn.T
            VT[:BLK, rows] = T3[j, 1, b * BLK : (b + 1) * BLK, :].T

        def clear(b, _):
            rows = span(b * KC, KC, KC)
            DK[rows, :] = jnp.zeros((KC, BLK), f32)
            DV[rows, :] = jnp.zeros((KC, BLK), f32)
            return 0

        lax.fori_loop(0, KEYS // KC, clear, 0)

        def chunks_of(q0):
            chunks = [span(q0 + KC * c, KC, KC) for c in range(4)]
            return chunks + [pl.ds(EXT + KC * c, KC) for c in range(TXT // KC)]

        def forward(u, k):
            q0 = u * QT
            qrows = span(q0, QT, QT)
            erows = span(SLAB + q0, QT, BLK)
            h = HX[j, erows, :].astype(f32)
            QA[k][:, :BLK] = ((h * RB[erows, :]) * gq).astype(bf16)
            for b in range(QT // BLK):
                bias = qb_ref[pl.ds(u * (QT // BLK) + b, 1), :].astype(bf16)
                QA[k][b * BLK : (b + 1) * BLK, BLK:] = jnp.broadcast_to(bias, (BLK, BLK))
            qa = QA[k][...]
            chunks = chunks_of(q0)
            top = None
            for c in range(NCHUNK):
                s = dot_nt(KA[chunks[c], :], qa)
                S[c] = s
                high = jnp.max(s, axis=0, keepdims=True)
                top = high if top is None else jnp.maximum(top, high)
                yield
            top = top * (SCALE * LOG2E)
            dt = DO[j, qrows, :].astype(f32).T
            ot = None
            for c in range(NCHUNK):
                p = jnp.exp2(S[c] * (SCALE * LOG2E) - top).astype(bf16)
                PB[k][c] = p
                term = dot_nn(VT[:, chunks[c]], p)
                ot = term if ot is None else ot + term
                yield
            inv = 1.0 / ot[BLK : BLK + 1, :]
            o = ot[:BLK, :] * inv
            delta = jnp.sum(dt * o, axis=0, keepdims=True) * inv
            DTS[k][...] = (dt * inv).astype(bf16)
            DL[k][...] = jnp.broadcast_to(delta, (8, QT))
            ATT[j, qrows, :] = o.T.astype(bf16)

        def backward(u, k):
            q0 = u * QT
            chunks = chunks_of(q0)
            dts = DTS[k][...]
            delta = DL[k][:1, :]
            qn = QA[k][:, :BLK]
            dq = None
            for c in range(NCHUNK):
                if c < 4:
                    v = HX[j, chunks[c], :]
                else:
                    v = T3[j, 1, (c - 4) * KC : (c - 3) * KC, :]
                p = PB[k][c]
                dp = dot_nn(v, dts)
                ds = (p.astype(f32) * (dp - delta)).astype(bf16)
                DV[chunks[c], :] += dot_nt(p, dts)
                yield
                DK[chunks[c], :] += dot_nn(ds, qn)
                term = dot_nn(KT[:, chunks[c]], ds)
                dq = term if dq is None else dq + term
                yield
            DQ[span(q0, QT, QT), :] = dq.T

        tiles = OWN // QT
        woven(forward(0, 0))

        def pair(v, _):
            woven(forward(2 * v + 1, 1), backward(2 * v, 0))
            woven(forward(2 * v + 2, 0), backward(2 * v + 1, 1))
            between(v)
            return 0

        lax.fori_loop(0, tiles // 2 - 1, pair, 0)
        woven(forward(tiles - 1, 1), backward(tiles - 2, 0))
        woven(backward(tiles - 1, 1))

        for d in ALL:
            cp_att(j, d).start()
        lo_att(j).start()

        for k in range(2):
            rows = slice(k * (OWN + SLAB), k * (OWN + SLAB) + SLAB)
            r = RB[rows, :]
            t = (gk * DK[rows, :]) * SCALE
            AH[j, k] = (DV[rows, :] + r * t).astype(bf16)
            MH[k] += (HX[j, rows, :].astype(f32) * r) * t
        for d in SIDES:
            cp_ah(j, d).start()
        TGP[j, 0] = (DK[EXT:, :] * SCALE).astype(bf16)
        TGP[j, 1] = DV[EXT:, :].astype(bf16)
        TG1[j, x] = TGP[j, :, block(x), :]
        for d in ALL:
            cp_rs(j, d).start()

        def own(i, _):
            rows = slab(i)
            qrows = oslab(i)
            r = RB[rows, :]
            t = (gq * DQ[qrows, :] + gk * DK[rows, :]) * SCALE
            AFS[par, qrows, :] = DV[rows, :] + r * t
            M[qrows, :] += (HX[j, rows, :].astype(f32) * r) * t
            return 0

        lax.fori_loop(0, NY, own, 0)

    def stage_d(j):
        par = lax.rem(j, 2)
        for d in SIDES:
            cp_ah(j, d, True).wait_recv()
        for i in range(NY):
            rows = slice(i * SLAB, (i + 1) * SLAB)
            a = AFS[par, rows, :]
            if i == 0:
                a = a + AHR[j, 0].astype(f32)
            if i == NY - 1:
                a = a + AHR[j, 1].astype(f32)
            AO[j, rows, :] = a.astype(bf16)
        for d in FOUR:
            cp_a(j, d).start()
        for d in ALL:
            cp_rs(j, d, True).wait_recv()
        for kv in range(2):
            total = TG1[j, 0, kv].astype(f32)
            for k in range(1, NX):
                total = total + TG1[j, k, kv].astype(f32)
            TG2[j, kv] = total.astype(bf16)
        TGY[j, :, block(y)] = TG2[j, 0]
        TGX[j, block(x), :] = TG2[j, 1]
        for d in ALL:
            cp_g1k(j, d).start()
            cp_g1v(j, d).start()

    def stage_e(j):
        for d in ALL:
            cp_g1k(j, d, True).wait_recv()
            cp_g1v(j, d, True).wait_recv()
        for d in SIDES:
            cp_g2k(j, d).start()
            cp_g2v(j, d).start()
        lo_g2k(j).start()
        lo_g2v(j).start()

    def stage_f(j):
        for d in SIDES:
            cp_g2k(j, d, True).wait_recv()
            cp_g3k(j, d).start()
            cp_g2v(j, d, True).wait_recv()
            cp_g3v(j, d).start()

    barrier = pltpu.get_barrier_semaphore()
    for d in ALL:
        pl.semaphore_signal(barrier, inc=1, device_id=yid(d), device_id_type=MESH)
        pl.semaphore_signal(barrier, inc=1, device_id=xid(d), device_id_type=MESH)
    for d in FOUR:
        pl.semaphore_signal(barrier, inc=1, device_id=above(d), device_id_type=MESH)
    load = pltpu.make_async_copy(hid, HS, loc1.at[0])
    load.start()

    def first_local(j, _):
        lo_h(j).start()
        lo_tx(j).start()
        lo_pass(j, 0).start()
        lo_pass(j, 1).start()
        lo_do(j).start()
        return 0

    lax.fori_loop(0, STEPS, first_local, 0)
    pl.semaphore_wait(barrier, 10)

    front(0)
    cp_hu().start()
    stage_p(0)

    lane = lax.broadcasted_iota(jnp.int32, (BLK, BLK), 1)

    def marks(b, _):
        KA[block(b), BLK:] = jnp.where(lane == b, 1.0, 0.0).astype(bf16)
        return 0

    lax.fori_loop(0, EXT // BLK, marks, 0)
    KA[EXT:, BLK:] = jnp.zeros((TXT, BLK), bf16)
    VT[BLK:, :] = jnp.ones((16, KEYS), bf16)

    def clear_m(i, _):
        M[oslab(i), :] = jnp.zeros((SLAB, BLK), f32)
        return 0

    lax.fori_loop(0, NY, clear_m, 0)
    for k in range(2):
        MH[k] = jnp.zeros((SLAB, BLK), f32)

    load.wait()

    for b in range(SLAB // BLK):
        h = HS[b * BLK : (b + 1) * BLK, :].astype(f32)
        mean = jnp.sum(h * h, axis=1, keepdims=True) * (1.0 / WIDTH)
        RT[8 * b : 8 * b + 8, :] = packed(lax.rsqrt(mean + EPS))[0]
    for d in ALL:
        cp_r(d).start()
    cp_ru().start()
    RTX[span(24 + 24 * y, 24, 8), :] = RT[...]
    for d in ALL:
        cp_r(d, True).wait_recv()
    for d in SIDES:
        cp_rh(d).start()
    for d in SIDES:
        cp_rh(d, True).wait_recv()
    stage_a(0)
    front(1)
    for b in range(EXT // BLK):
        RB[b * BLK : (b + 1) * BLK, :] = unpacked(RTX[8 * b : 8 * b + 8, :])
    stage_b(0)
    stage_p(1)
    front(2)
    stage_a(1)
    front(3)

    def step(j, _):
        def between(v):
            @pl.when((v == 0) & (j + 1 < STEPS))
            def _():
                stage_b(j + 1)

            @pl.when((v == 0) & (j + 2 < STEPS))
            def _():
                stage_p(j + 2)

            @pl.when((v == 1) & (j + 2 < STEPS))
            def _():
                stage_a(j + 2)

            @pl.when((v == 1) & (j + 4 < STEPS))
            def _():
                front(j + 4)

        stage_c(j, between)

        @pl.when(j >= 1)
        def _():
            stage_d(j - 1)

        @pl.when(j >= 2)
        def _():
            stage_e(j - 2)

        @pl.when(j >= 3)
        def _():
            stage_f(j - 3)

        return 0

    lax.fori_loop(0, STEPS, step, 0)

    for k in range(2):
        tiles = packed(jnp.sum(MH[k], axis=1, keepdims=True))
        for b in range(SLAB // BLK):
            MHS[k, 8 * b : 8 * b + 8, :] = tiles[b]
    for d in SIDES:
        cp_mh(d).start()
    stage_d(STEPS - 1)
    stage_e(STEPS - 2)
    for b in range(OWN // BLK):
        column = jnp.sum(M[b * BLK : (b + 1) * BLK, :], axis=1, keepdims=True)
        MT[8 * b : 8 * b + 8, :] = packed(column)[0]
    for d in SIDES:
        cp_mh(d, True).wait_recv()
    MT[:24, :] += MHR[0]
    MT[72:96, :] += MHR[1]
    for d in FOUR:
        cp_m(d).start()
    stage_e(STEPS - 1)
    stage_f(STEPS - 3)
    stage_f(STEPS - 2)
    cp_hu().wait_recv()
    cp_ru().wait_recv()
    for d in FOUR:
        cp_m(d, True).wait_recv()

    def arrived(j, _):
        for d in FOUR:
            cp_a(j, d, True).wait_recv()
        return 0

    lax.fori_loop(0, STEPS, arrived, 0)
    for b in range(SLAB // BLK):
        rows = slice(b * BLK, (b + 1) * BLK)
        tiles = slice(8 * b, 8 * b + 8)
        mean = (MR[0, tiles] + MR[1, tiles] + MR[2, tiles] + MR[3, tiles]) * (1.0 / WIDTH)
        r = RU[tiles, :]
        factor = unpacked(mean * (r * r))[:, :1]
        grad = AF[rows, :].astype(f32) - HU[rows, :].astype(f32) * factor
        DH[rows, :] = jnp.where(section < sections - 1, grad, 0.0).astype(bf16)
    store = pltpu.make_async_copy(DH, dh_out, loc1.at[1])
    store.start()
    stage_f(STEPS - 1)
    store.wait()

    def last(j, _):
        for d in ALL:
            cp_att(j, d, True).wait_recv()
            for copy in (cp_h, cp_do, cp_ty, cp_tg, cp_att, cp_rs, cp_g1k, cp_g1v):
                copy(j, d).wait_send()
        for d in FOUR:
            cp_a(j, d).wait_send()
        for d in SIDES:
            cp_g3k(j, d, True).wait_recv()
            cp_g3v(j, d, True).wait_recv()
            for copy in (cp_g2k, cp_g2v, cp_g3k, cp_g3v):
                copy(j, d).wait_send()
            cp_tx_far(j, d).wait_send()
            cp_tx_near(j, d).wait_send()
            cp_tx_pass(j, d).wait_send()
            cp_halo(j, d).wait_send()
            cp_ah(j, d).wait_send()
        lo_att(j).wait()
        lo_g2k(j).wait()
        lo_g2v(j).wait()
        return 0

    lax.fori_loop(0, STEPS, last, 0)
    for d in ALL:
        cp_r(d).wait_send()
    for d in FOUR:
        cp_m(d).wait_send()
    cp_hu().wait_send()
    cp_ru().wait_send()
    for d in SIDES:
        cp_rh(d).wait_send()
        cp_mh(d).wait_send()


def query_bias(pattern, x):
    blocks = OWN // BLK
    reach = SLAB // BLK
    span_ = pattern.shape[1]
    rows = lax.dynamic_slice_in_dim(pattern, x * blocks, blocks, 0)
    first = jnp.arange(blocks, dtype=jnp.int32)[:, None]
    col = jnp.arange(BLK, dtype=jnp.int32)[None, :]
    offset = col - first
    picked = sum(jnp.where(offset == k, rows[:, k : k + 1], 0) for k in range(span_))
    globe = x * blocks - reach + col
    inside = (globe >= 0) & (globe < pattern.shape[0])
    allowed = ((picked > 0) & inside) | (col >= EXT // BLK)
    return jnp.where(allowed, 0.0, NEG).astype(f32)


def local(hidden, query_norm_gain, key_norm_gain, text_kv, holder, pattern, grad_out):
    x = lax.axis_index("seq") // NY
    qbias = query_bias(pattern, x)
    who = holder[0]
    row = lax.broadcasted_iota(jnp.int32, (NX + NY, NY * BLK), 0)
    select = jnp.where(row < NX, row == (who // NY - x + NX) % NX, row - NX == who % NY).astype(f32)
    any_spec = pl.BlockSpec(memory_space=pl.ANY)
    vmem = pl.BlockSpec(memory_space=pltpu.VMEM)

    def V(*shape, dtype=bf16):
        return pltpu.VMEM(shape, dtype)

    attended, upstream, text_total = pl.pallas_call(
        kernel,
        out_shape=(
            jax.ShapeDtypeStruct((SLAB, WIDTH), bf16),
            jax.ShapeDtypeStruct((SLAB, WIDTH), bf16),
            jax.ShapeDtypeStruct((2, TXT, WIDTH), bf16),
        ),
        in_specs=[any_spec] * 3 + [vmem] * 4,
        out_specs=[any_spec] * 3,
        scratch_shapes=[
            V(SLAB, WIDTH),
            V(SLAB, WIDTH),
            V(24, BLK, dtype=f32),
            V(STEPS, EXT, BLK),
            V(STEPS, OWN, BLK),
            V(EXT // BLK * 8, BLK, dtype=f32),
            V(24, BLK, dtype=f32),
            V(EXT, BLK, dtype=f32),
            V(STEPS, 2, BLK, NY * BLK),
            V(STEPS, 2, BLK, NY * BLK),
            V(STEPS, 2, BLK, NY * BLK),
            V(STEPS, 3, 2, BLK, NY * BLK),
            V(STEPS, 2, BLK, NY * BLK),
            V(STEPS, NY, 2, BLK, BLK),
            V(STEPS, 2, TXT, BLK),
            V(KEYS, 2 * BLK),
            V(BLK, KEYS),
            V(BLK + 16, KEYS),
            V(QT, 2 * BLK),
            V(QT, 2 * BLK),
            V(NCHUNK, KC, QT, dtype=f32),
            V(NCHUNK, KC, QT),
            V(NCHUNK, KC, QT),
            V(BLK, QT),
            V(BLK, QT),
            V(8, QT, dtype=f32),
            V(8, QT, dtype=f32),
            V(KEYS, BLK, dtype=f32),
            V(KEYS, BLK, dtype=f32),
            V(OWN, BLK, dtype=f32),
            V(STEPS, OWN, BLK),
            V(2, OWN, BLK, dtype=f32),
            V(STEPS, 2, SLAB, BLK),
            V(STEPS, 2, SLAB, BLK),
            V(STEPS, OWN, BLK),
            V(SLAB, WIDTH),
            V(OWN, BLK, dtype=f32),
            V(2, SLAB, BLK, dtype=f32),
            V(96, BLK, dtype=f32),
            V(2, 24, BLK, dtype=f32),
            V(2, 24, BLK, dtype=f32),
            V(NY, 24, BLK, dtype=f32),
            V(STEPS, 2, TXT, BLK),
            V(STEPS, NX, 2, BLK, BLK),
            V(STEPS, 2, BLK, BLK),
            V(STEPS, BLK, NY * BLK),
            V(STEPS, TXT, BLK),
            V(SLAB, WIDTH),
            pltpu.SemaphoreType.DMA((KINDS, STEPS, 8)),
            pltpu.SemaphoreType.DMA((KINDS, STEPS, 8)),
            pltpu.SemaphoreType.DMA((5, 4)),
            pltpu.SemaphoreType.DMA((5, 4)),
            pltpu.SemaphoreType.DMA((8, STEPS)),
            pltpu.SemaphoreType.DMA((2,)),
        ],
        compiler_params=pltpu.CompilerParams(
            collective_id=0, has_side_effects=True, vmem_limit_bytes=60 * 1024 * 1024
        ),
        cost_estimate=pl.CostEstimate(
            flops=24 * 10**9, bytes_accessed=40 * 10**6, transcendentals=12 * 10**6
        ),
        name="attention",
    )(
        hidden[0],
        grad_out[0],
        text_kv[0, 0],
        query_norm_gain,
        key_norm_gain,
        select,
        qbias,
    )
    return (attended[None], upstream[None], text_total[None])


def solution(mesh):
    in_specs = (
        P("section", "seq", None),
        P("section", None),
        P("section", None),
        P("section", "seq", None, None, None),
        P("section"),
        P(),
        P("section", "seq", None),
    )
    out_specs = (
        P("section", "seq", None),
        P("section", "seq", None),
        P("section", None, None, None),
    )
    return jax.shard_map(local, mesh=mesh, in_specs=in_specs, out_specs=out_specs, check_vma=False)
```

```python
import jax
import jax.numpy as jnp
from jax import lax
from jax.experimental import pallas as pl
from jax.experimental.pallas import tpu as pltpu
from jax.sharding import PartitionSpec as P

HDIM = 128
BLK = 128
EPS = 1e-06
MESH = pl.DeviceIdType.MESH

NX = 4
NY = 4
SLAB = 384
TXT = 512
WIDTH = 2560
STEPS = 5
OWN = NY * SLAB
EXT = OWN + 2 * SLAB
KEYS = EXT + TXT
QT = 256
KC = 256
NCHUNK = 4 + TXT // KC
SCALE = HDIM ** (-0.5)
LOG2E = 1.4426950408889634
NEG = -1e30

(
    K_H,
    K_DO,
    K_TX,
    K_TY,
    K_TG,
    K_HALO,
    K_ATT,
    K_AH,
    K_A,
    K_RS,
    K_G1,
    K_G2,
    K_G3,
) = range(13)
KINDS = 13
O_R, O_RH, O_MH, O_M, O_HU = range(5)

f32 = jnp.float32
bf16 = jnp.bfloat16


def dot_nn(a, b):
    return lax.dot_general(a, b, (((1,), (0,)), ((), ())), preferred_element_type=f32)


def dot_nt(a, b):
    return lax.dot_general(a, b, (((1,), (1,)), ((), ())), preferred_element_type=f32)


def woven(*parts):
    parts = list(parts)
    while parts:
        for part in list(parts):
            if next(part, True):
                parts.remove(part)


def block(k):
    return pl.ds(pl.multiple_of(k * BLK, BLK), BLK)


def span(start, size, unit):
    return pl.ds(pl.multiple_of(start, unit), size)


def packed(column):
    rows = column.shape[0]
    wide = jnp.broadcast_to(column, (rows, BLK))
    return [wide[b * BLK : (b + 1) * BLK].T[:8] for b in range(rows // BLK)]


def unpacked(tile):
    return jnp.broadcast_to(tile[:1], (BLK, BLK)).T


def kernel(
    hid, do_in, txt, gq_ref, gk_ref, sel_ref, qb_ref,
    att_out, dh_out, tg_out,
    HS, HU, RU, HX, DO, RTX, RT, RB, TP, TQ, TM, T1, TS, T2, T3, KA, KT, VT, QA0, QA1, S, PB0, PB1, DTS0, DTS1, DL0, DL1, DK, DV, DQ,
    ATT, AFS, AH, AHR, AO, AF, M, MH, MT, MHS, MHR, MR, TGP, TG1, TG2, TGY, TGX, DH,
    send, recv, once_send, once_recv, loc, loc1,
):
    QA, PB, DTS, DL = (QA0, QA1), (PB0, PB1), (DTS0, DTS1), (DL0, DL1)
    seq = lax.axis_index("seq")
    section = lax.axis_index("section")
    sections = lax.axis_size("section")
    x = lax.div(seq, NY)
    y = lax.rem(seq, NY)

    def ry(d):
        return lax.rem(y + (d + NY), NY)

    def rx(d):
        return lax.rem(x + (d + NX), NX)

    def yid(d):
        return {"seq": x * NY + ry(d)}

    def xid(d):
        return {"seq": rx(d) * NY + y}

    def below(d):
        return {"seq": x * NY + ry(d), "section": lax.rem(section + (sections - 1), sections)}

    def above(d):
        return {"seq": x * NY + ry(d), "section": lax.rem(section + 1, sections)}

    def rc(src, dst, kind, j, d, dev):
        return pltpu.make_async_remote_copy(
            src_ref=src, dst_ref=dst, send_sem=send.at[kind, j, d],
            recv_sem=recv.at[kind, j, d], device_id=dev, device_id_type=MESH,
        )

    def rc1(src, dst, kind, d, dev):
        return pltpu.make_async_remote_copy(
            src_ref=src, dst_ref=dst, send_sem=once_send.at[kind, d],
            recv_sem=once_recv.at[kind, d], device_id=dev, device_id_type=MESH,
        )

    def hcol(j, yy):
        return block(NY * j + yy)

    def wide(j):
        return span(j * (NY * BLK), NY * BLK, NY * BLK)

    def slab(yy):
        return span(SLAB + SLAB * yy, SLAB, SLAB)

    def oslab(yy):
        return span(SLAB * yy, SLAB, SLAB)

    def cp_h(j, d, w=False):
        return rc(hid.at[:, hcol(j, ry(d))], HX.at[j, slab(ry(-d) if w else y), :], K_H, j, d, yid(d))

    def cp_do(j, d, w=False):
        return rc(do_in.at[:, hcol(j, ry(d))], DO.at[j, oslab(ry(-d) if w else y), :], K_DO, j, d, yid(d))

    def cp_tx_far(j, d, w=False):
        kv = 0 if d == 1 else 1
        return rc(txt.at[kv, block(rx(2)), wide(j)], TP.at[j, kv], K_TX, j, d, xid(d))

    def cp_tx_near(j, d, w=False):
        side, kv = (0, 1) if d == 1 else (1, 0)
        return rc(txt.at[kv, block(rx(d)), wide(j)], T1.at[j, side, kv], K_TX, j, 4 + d, xid(d))

    def cp_tx_pass(j, d, w=False):
        kv = 0 if d == 1 else 1
        return rc(TM.at[j, kv], T1.at[j, kv, kv], K_TX, j, 1 + d, xid(d))

    def cp_ty(j, d, w=False):
        return rc(TS.at[j, :, :, block(ry(d))], T2.at[j, ry(-d) if w else y], K_TY, j, d, yid(d))

    def cp_tg(j, d, w=False):
        return rc(T3.at[j, :, block(x), :], T3.at[j, :, block(rx(-d) if w else x), :], K_TG, j, d, xid(d))

    def cp_halo(j, d, w=False):
        if d == 1:
            return rc(HX.at[j, pl.ds(OWN, SLAB), :], HX.at[j, pl.ds(0, SLAB), :], K_HALO, j, 1, xid(1))
        return rc(HX.at[j, pl.ds(SLAB, SLAB), :], HX.at[j, pl.ds(OWN + SLAB, SLAB), :], K_HALO, j, 3, xid(3))

    def cp_att(j, d, w=False):
        return rc(ATT.at[j, oslab(ry(d)), :], att_out.at[:, hcol(j, ry(-d) if w else y)], K_ATT, j, d, yid(d))

    def cp_ah(j, d, w=False):
        k = 1 if d == 1 else 0
        return rc(AH.at[j, k], AHR.at[j, 1 - k], K_AH, j, d, xid(d))

    def cp_a(j, d, w=False):
        return rc(AO.at[j, oslab(ry(d)), :], AF.at[:, hcol(j, ry(-d) if w else y)], K_A, j, d, below(d))

    def cp_rs(j, d, w=False):
        return rc(TGP.at[j, :, block(rx(d)), :], TG1.at[j, rx(-d) if w else x], K_RS, j, d, xid(d))

    def cp_g1k(j, d, w=False):
        return rc(TG2.at[j, 0], TGY.at[j, :, block(ry(-d) if w else y)], K_G1, j, d, yid(d))

    def cp_g1v(j, d, w=False):
        return rc(TG2.at[j, 1], TGX.at[j, block(rx(-d) if w else x), :], K_G1, j, 4 + d, xid(d))

    def cp_g2k(j, d, w=False):
        return rc(TGY.at[j], tg_out.at[0, block(rx(-d) if w else x), wide(j)], K_G2, j, d, xid(d))

    def cp_g2v(j, d, w=False):
        return rc(TGX.at[j], tg_out.at[1, :, hcol(j, ry(-d) if w else y)], K_G2, j, 4 + d, yid(d))

    def cp_g3k(j, d, w=False):
        part = 0 if d == 1 else 1
        who = rx(2) if w else rx(-d)
        half = BLK // 2
        rows = span(who * BLK + part * half, half, half)
        return rc(tg_out.at[0, rows, wide(j)], tg_out.at[0, rows, wide(j)], K_G3, j, d, xid(d))

    def cp_g3v(j, d, w=False):
        part = 0 if d == 1 else 1
        who = ry(2) if w else ry(-d)
        rows = pl.ds(part * (TXT // 2), TXT // 2)
        return rc(tg_out.at[1, rows, hcol(j, who)], tg_out.at[1, rows, hcol(j, who)], K_G3, j, 4 + d, yid(d))

    def cp_r(d, w=False):
        return rc1(RT, RTX.at[span(24 + 24 * (ry(-d) if w else y), 24, 8), :], O_R, d, yid(d))

    def cp_rh(d, w=False):
        if d == 1:
            return rc1(RTX.at[pl.ds(96, 24), :], RTX.at[pl.ds(0, 24), :], O_RH, 1, xid(1))
        return rc1(RTX.at[pl.ds(24, 24), :], RTX.at[pl.ds(120, 24), :], O_RH, 3, xid(3))

    def cp_mh(d, w=False):
        k = 1 if d == 1 else 0
        return rc1(MHS.at[k], MHR.at[1 - k], O_MH, d, xid(d))

    def cp_m(d, w=False):
        return rc1(MT.at[span(24 * ry(d), 24, 8), :], MR.at[ry(-d) if w else y], O_M, d, below(d))

    def cp_hu():
        return rc1(hid, HU, O_HU, 0, below(0))

    def cp_ru():
        return rc1(RT, RU, O_HU, 1, below(0))

    def lo_h(j):
        return pltpu.make_async_copy(hid.at[:, hcol(j, y)], HX.at[j, slab(y), :], loc.at[0, j])

    def lo_do(j):
        return pltpu.make_async_copy(do_in.at[:, hcol(j, y)], DO.at[j, oslab(y), :], loc.at[1, j])

    def lo_tx(j):
        return pltpu.make_async_copy(txt.at[:, block(x), wide(j)], T1.at[j, 2], loc.at[2, j])

    def lo_pass(j, kv):
        where = rx(1) if kv == 0 else rx(-1)
        return pltpu.make_async_copy(txt.at[kv, block(where), wide(j)], TQ.at[j, kv], loc.at[6 + kv, j])

    def lo_att(j):
        return pltpu.make_async_copy(ATT.at[j, oslab(y), :], att_out.at[:, hcol(j, y)], loc.at[3, j])

    def lo_g2k(j):
        return pltpu.make_async_copy(TGY.at[j], tg_out.at[0, block(x), wide(j)], loc.at[4, j])

    def lo_g2v(j):
        return pltpu.make_async_copy(TGX.at[j], tg_out.at[1, :, hcol(j, y)], loc.at[5, j])

    ALL = (1, 3, 2)
    FOUR = (0, 1, 3, 2)
    SIDES = (1, 3)

    def front(j):
        for d in SIDES:
            cp_tx_far(j, d).start()
        for d in SIDES:
            cp_tx_near(j, d).start()
        for d in ALL:
            cp_h(j, d).start()
        for d in ALL:
            cp_do(j, d).start()

    def stage_p(j):
        for kv in range(2):
            lo_pass(j, kv).wait()
            cp_tx_far(j, 1 if kv == 0 else 3, True).wait_recv()
            far = sel_ref[3:4, :] if kv == 0 else sel_ref[1:2, :]
            part = TP[j, kv].astype(f32) * far + TQ[j, kv].astype(f32) * (1.0 - far)
            TM[j, kv] = part.astype(bf16)
            cp_tx_pass(j, 1 if kv == 0 else 3).start()

    def stage_a(j):
        lo_tx(j).wait()
        for d in SIDES:
            cp_tx_near(j, d, True).wait_recv()
            cp_tx_pass(j, d, True).wait_recv()
        here, up, two, down = (sel_ref[k : k + 1, :] for k in range(NX))
        for kv in range(2):
            low, high = (down + two, up) if kv == 0 else (down, up + two)
            part = T1[j, 2, kv].astype(f32) * here
            part = part + T1[j, 0, kv].astype(f32) * low
            part = part + T1[j, 1, kv].astype(f32) * high
            TS[j, kv] = part.astype(bf16)
        T2[j, y] = TS[j, :, :, block(y)]
        for d in ALL:
            cp_ty(j, d).start()
        lo_h(j).wait()
        for d in ALL:
            cp_h(j, d, True).wait_recv()
        for d in SIDES:
            cp_halo(j, d).start()

    def stage_b(j):
        for d in ALL:
            cp_ty(j, d, True).wait_recv()
        for kv in range(2):
            part = jnp.zeros((BLK, BLK), f32)
            for k in range(NY):
                part = part + T2[j, k, kv].astype(f32) * sel_ref[NX + k : NX + k + 1, :BLK]
            T3[j, kv, block(x), :] = part.astype(bf16)
        for d in ALL:
            cp_tg(j, d).start()

    def send_att(j):
        for d in ALL:
            cp_att(j, d).start()
        lo_att(j).start()

    def stage_c(j, between):
        for d in SIDES:
            cp_halo(j, d, True).wait_recv()
        lo_do(j).wait()
        for d in ALL:
            cp_do(j, d, True).wait_recv()
            cp_tg(j, d, True).wait_recv()
        gq = gq_ref[:, hcol(j, y)]
        gk = gk_ref[:, hcol(j, y)]
        par = lax.rem(j, 2)

        def prep(b, _):
            rows = block(b)
            h = HX[j, rows, :].astype(f32)
            kn = (h * RB[rows, :]) * gk
            KA[rows, :BLK] = kn.astype(bf16)
            KT[:, rows] = kn.astype(bf16).T
            VT[:BLK, rows] = HX[j, rows, :].T
            return 0

        lax.fori_loop(0, EXT // BLK, prep, 0)
        for b in range(TXT // BLK):
            rows = slice(EXT + b * BLK, EXT + (b + 1) * BLK)
            kn = T3[j, 0, b * BLK : (b + 1) * BLK, :]
            KA[rows, :BLK] = kn
            KT[:, rows] = kn.T
            VT[:BLK, rows] = T3[j, 1, b * BLK : (b + 1) * BLK, :].T

        def clear(b, _):
            rows = span(b * KC, KC, KC)
            DK[rows, :] = jnp.zeros((KC, BLK), f32)
            DV[rows, :] = jnp.zeros((KC, BLK), f32)
            return 0

        lax.fori_loop(0, KEYS // KC, clear, 0)

        def chunks_of(q0):
            chunks = [span(q0 + KC * c, KC, KC) for c in range(4)]
            return chunks + [pl.ds(EXT + KC * c, KC) for c in range(TXT // KC)]

        def forward(u, k):
            q0 = u * QT
            qrows = span(q0, QT, QT)
            erows = span(SLAB + q0, QT, BLK)
            h = HX[j, erows, :].astype(f32)
            QA[k][:, :BLK] = ((h * RB[erows, :]) * gq).astype(bf16)
            for b in range(QT // BLK):
                bias = qb_ref[pl.ds(u * (QT // BLK) + b, 1), :].astype(bf16)
                QA[k][b * BLK : (b + 1) * BLK, BLK:] = jnp.broadcast_to(bias, (BLK, BLK))
            qa = QA[k][...]
            chunks = chunks_of(q0)
            top = None
            for c in range(NCHUNK):
                s = dot_nt(KA[chunks[c], :], qa)
                S[c] = s
                high = jnp.max(s, axis=0, keepdims=True)
                top = high if top is None else jnp.maximum(top, high)
                yield
            top = top * (SCALE * LOG2E)
            dt = DO[j, qrows, :].astype(f32).T
            ot = None
            for c in range(NCHUNK):
                p = jnp.exp2(S[c] * (SCALE * LOG2E) - top).astype(bf16)
                PB[k][c] = p
                term = dot_nn(VT[:, chunks[c]], p)
                ot = term if ot is None else ot + term
                yield
            inv = 1.0 / ot[BLK : BLK + 1, :]
            o = ot[:BLK, :] * inv
            delta = jnp.sum(dt * o, axis=0, keepdims=True) * inv
            DTS[k][...] = (dt * inv).astype(bf16)
            DL[k][...] = jnp.broadcast_to(delta, (8, QT))
            ATT[j, qrows, :] = o.T.astype(bf16)

        def backward(u, k):
            q0 = u * QT
            chunks = chunks_of(q0)
            dts = DTS[k][...]
            delta = DL[k][:1, :]
            qn = QA[k][:, :BLK]
            dq = None
            for c in range(NCHUNK):
                if c < 4:
                    v = HX[j, chunks[c], :]
                else:
                    v = T3[j, 1, (c - 4) * KC : (c - 3) * KC, :]
                p = PB[k][c]
                dp = dot_nn(v, dts)
                ds = (p.astype(f32) * (dp - delta)).astype(bf16)
                DV[chunks[c], :] += dot_nt(p, dts)
                yield
                DK[chunks[c], :] += dot_nn(ds, qn)
                term = dot_nn(KT[:, chunks[c]], ds)
                dq = term if dq is None else dq + term
                yield
            DQ[span(q0, QT, QT), :] = dq.T

        tiles = OWN // QT
        woven(forward(0, 0))

        def pair(v, _):
            woven(forward(2 * v + 1, 1), backward(2 * v, 0))
            woven(forward(2 * v + 2, 0), backward(2 * v + 1, 1))
            between(v)
            return 0

        lax.fori_loop(0, tiles // 2 - 1, pair, 0)
        woven(forward(tiles - 1, 1), backward(tiles - 2, 0))
        woven(backward(tiles - 1, 1))

        @pl.when(j < STEPS - 1)
        def _():
            send_att(j)

        for k in range(2):
            rows = slice(k * (OWN + SLAB), k * (OWN + SLAB) + SLAB)
            r = RB[rows, :]
            t = (gk * DK[rows, :]) * SCALE
            AH[j, k] = (DV[rows, :] + r * t).astype(bf16)
            MH[k] += (HX[j, rows, :].astype(f32) * r) * t
        for d in SIDES:
            cp_ah(j, d).start()
        TGP[j, 0] = (DK[EXT:, :] * SCALE).astype(bf16)
        TGP[j, 1] = DV[EXT:, :].astype(bf16)
        TG1[j, x] = TGP[j, :, block(x), :]
        for d in ALL:
            cp_rs(j, d).start()

        def own(i, _):
            rows = slab(i)
            qrows = oslab(i)
            r = RB[rows, :]
            t = (gq * DQ[qrows, :] + gk * DK[rows, :]) * SCALE
            AFS[par, qrows, :] = DV[rows, :] + r * t
            M[qrows, :] += (HX[j, rows, :].astype(f32) * r) * t
            return 0

        lax.fori_loop(0, NY, own, 0)

    def stage_d(j):
        par = lax.rem(j, 2)
        for d in SIDES:
            cp_ah(j, d, True).wait_recv()
        for i in range(NY):
            rows = slice(i * SLAB, (i + 1) * SLAB)
            a = AFS[par, rows, :]
            if i == 0:
                a = a + AHR[j, 0].astype(f32)
            if i == NY - 1:
                a = a + AHR[j, 1].astype(f32)
            AO[j, rows, :] = a.astype(bf16)
        for d in FOUR:
            cp_a(j, d).start()
        for d in ALL:
            cp_rs(j, d, True).wait_recv()
        for kv in range(2):
            total = TG1[j, 0, kv].astype(f32)
            for k in range(1, NX):
                total = total + TG1[j, k, kv].astype(f32)
            TG2[j, kv] = total.astype(bf16)
        TGY[j, :, block(y)] = TG2[j, 0]
        TGX[j, block(x), :] = TG2[j, 1]
        for d in ALL:
            cp_g1k(j, d).start()
            cp_g1v(j, d).start()

    def stage_e(j):
        for d in ALL:
            cp_g1k(j, d, True).wait_recv()
            cp_g1v(j, d, True).wait_recv()
        for d in SIDES:
            cp_g2k(j, d).start()
            cp_g2v(j, d).start()
        lo_g2k(j).start()
        lo_g2v(j).start()

    def stage_f(j):
        for d in SIDES:
            cp_g2k(j, d, True).wait_recv()
            cp_g3k(j, d).start()
            cp_g2v(j, d, True).wait_recv()
            cp_g3v(j, d).start()

    barrier = pltpu.get_barrier_semaphore()
    for d in ALL:
        pl.semaphore_signal(barrier, inc=1, device_id=yid(d), device_id_type=MESH)
        pl.semaphore_signal(barrier, inc=1, device_id=xid(d), device_id_type=MESH)
    for d in FOUR:
        pl.semaphore_signal(barrier, inc=1, device_id=above(d), device_id_type=MESH)
    load = pltpu.make_async_copy(hid, HS, loc1.at[0])
    load.start()

    def first_local(j, _):
        lo_h(j).start()
        lo_tx(j).start()
        lo_pass(j, 0).start()
        lo_pass(j, 1).start()
        lo_do(j).start()
        return 0

    lax.fori_loop(0, STEPS, first_local, 0)
    pl.semaphore_wait(barrier, 10)

    front(0)
    cp_hu().start()
    stage_p(0)

    lane = lax.broadcasted_iota(jnp.int32, (BLK, BLK), 1)

    def marks(b, _):
        KA[block(b), BLK:] = jnp.where(lane == b, 1.0, 0.0).astype(bf16)
        return 0

    lax.fori_loop(0, EXT // BLK, marks, 0)
    KA[EXT:, BLK:] = jnp.zeros((TXT, BLK), bf16)
    VT[BLK:, :] = jnp.ones((16, KEYS), bf16)

    def clear_m(i, _):
        M[oslab(i), :] = jnp.zeros((SLAB, BLK), f32)
        return 0

    lax.fori_loop(0, NY, clear_m, 0)
    for k in range(2):
        MH[k] = jnp.zeros((SLAB, BLK), f32)

    load.wait()

    for b in range(SLAB // BLK):
        h = HS[b * BLK : (b + 1) * BLK, :].astype(f32)
        mean = jnp.sum(h * h, axis=1, keepdims=True) * (1.0 / WIDTH)
        RT[8 * b : 8 * b + 8, :] = packed(lax.rsqrt(mean + EPS))[0]
    for d in ALL:
        cp_r(d).start()
    cp_ru().start()
    RTX[span(24 + 24 * y, 24, 8), :] = RT[...]
    for d in ALL:
        cp_r(d, True).wait_recv()
    for d in SIDES:
        cp_rh(d).start()
    for d in SIDES:
        cp_rh(d, True).wait_recv()
    stage_a(0)
    front(1)
    for b in range(EXT // BLK):
        RB[b * BLK : (b + 1) * BLK, :] = unpacked(RTX[8 * b : 8 * b + 8, :])
    stage_b(0)
    stage_p(1)
    front(2)
    stage_a(1)
    front(3)

    def step(j, _):
        def between(v):
            @pl.when((v == 0) & (j + 1 < STEPS))
            def _():
                stage_b(j + 1)

            @pl.when((v == 0) & (j + 2 < STEPS))
            def _():
                stage_p(j + 2)

            @pl.when((v == 1) & (j + 2 < STEPS))
            def _():
                stage_a(j + 2)

            @pl.when((v == 1) & (j + 4 < STEPS))
            def _():
                front(j + 4)

        stage_c(j, between)

        @pl.when(j >= 1)
        def _():
            stage_d(j - 1)

        @pl.when(j >= 2)
        def _():
            stage_e(j - 2)

        @pl.when(j >= 3)
        def _():
            stage_f(j - 3)

        return 0

    lax.fori_loop(0, STEPS, step, 0)

    for k in range(2):
        tiles = packed(jnp.sum(MH[k], axis=1, keepdims=True))
        for b in range(SLAB // BLK):
            MHS[k, 8 * b : 8 * b + 8, :] = tiles[b]
    for d in SIDES:
        cp_mh(d).start()
    stage_d(STEPS - 1)
    send_att(STEPS - 1)
    stage_e(STEPS - 2)
    for b in range(OWN // BLK):
        column = jnp.sum(M[b * BLK : (b + 1) * BLK, :], axis=1, keepdims=True)
        MT[8 * b : 8 * b + 8, :] = packed(column)[0]
    for d in SIDES:
        cp_mh(d, True).wait_recv()
    MT[:24, :] += MHR[0]
    MT[72:96, :] += MHR[1]
    for d in FOUR:
        cp_m(d).start()
    stage_e(STEPS - 1)
    stage_f(STEPS - 3)
    stage_f(STEPS - 2)
    cp_hu().wait_recv()
    cp_ru().wait_recv()
    for d in FOUR:
        cp_m(d, True).wait_recv()

    def arrived(j, _):
        for d in FOUR:
            cp_a(j, d, True).wait_recv()
        return 0

    lax.fori_loop(0, STEPS, arrived, 0)
    for b in range(SLAB // BLK):
        rows = slice(b * BLK, (b + 1) * BLK)
        tiles = slice(8 * b, 8 * b + 8)
        mean = (MR[0, tiles] + MR[1, tiles] + MR[2, tiles] + MR[3, tiles]) * (1.0 / WIDTH)
        r = RU[tiles, :]
        factor = unpacked(mean * (r * r))[:, :1]
        grad = AF[rows, :].astype(f32) - HU[rows, :].astype(f32) * factor
        DH[rows, :] = jnp.where(section < sections - 1, grad, 0.0).astype(bf16)
    store = pltpu.make_async_copy(DH, dh_out, loc1.at[1])
    store.start()
    stage_f(STEPS - 1)
    store.wait()

    def last(j, _):
        for d in ALL:
            cp_att(j, d, True).wait_recv()
            for copy in (cp_h, cp_do, cp_ty, cp_tg, cp_att, cp_rs, cp_g1k, cp_g1v):
                copy(j, d).wait_send()
        for d in FOUR:
            cp_a(j, d).wait_send()
        for d in SIDES:
            cp_g3k(j, d, True).wait_recv()
            cp_g3v(j, d, True).wait_recv()
            for copy in (cp_g2k, cp_g2v, cp_g3k, cp_g3v):
                copy(j, d).wait_send()
            cp_tx_far(j, d).wait_send()
            cp_tx_near(j, d).wait_send()
            cp_tx_pass(j, d).wait_send()
            cp_halo(j, d).wait_send()
            cp_ah(j, d).wait_send()
        lo_att(j).wait()
        lo_g2k(j).wait()
        lo_g2v(j).wait()
        return 0

    lax.fori_loop(0, STEPS, last, 0)
    for d in ALL:
        cp_r(d).wait_send()
    for d in FOUR:
        cp_m(d).wait_send()
    cp_hu().wait_send()
    cp_ru().wait_send()
    for d in SIDES:
        cp_rh(d).wait_send()
        cp_mh(d).wait_send()


def query_bias(pattern, x):
    blocks = OWN // BLK
    reach = SLAB // BLK
    span_ = pattern.shape[1]
    rows = lax.dynamic_slice_in_dim(pattern, x * blocks, blocks, 0)
    first = jnp.arange(blocks, dtype=jnp.int32)[:, None]
    col = jnp.arange(BLK, dtype=jnp.int32)[None, :]
    offset = col - first
    picked = sum(jnp.where(offset == k, rows[:, k : k + 1], 0) for k in range(span_))
    globe = x * blocks - reach + col
    inside = (globe >= 0) & (globe < pattern.shape[0])
    allowed = ((picked > 0) & inside) | (col >= EXT // BLK)
    return jnp.where(allowed, 0.0, NEG).astype(f32)


def local(hidden, query_norm_gain, key_norm_gain, text_kv, holder, pattern, grad_out):
    x = lax.axis_index("seq") // NY
    qbias = query_bias(pattern, x)
    who = holder[0]
    row = lax.broadcasted_iota(jnp.int32, (NX + NY, NY * BLK), 0)
    select = jnp.where(row < NX, row == (who // NY - x + NX) % NX, row - NX == who % NY).astype(f32)
    any_spec = pl.BlockSpec(memory_space=pl.ANY)
    vmem = pl.BlockSpec(memory_space=pltpu.VMEM)

    def V(*shape, dtype=bf16):
        return pltpu.VMEM(shape, dtype)

    attended, upstream, text_total = pl.pallas_call(
        kernel,
        out_shape=(
            jax.ShapeDtypeStruct((SLAB, WIDTH), bf16),
            jax.ShapeDtypeStruct((SLAB, WIDTH), bf16),
            jax.ShapeDtypeStruct((2, TXT, WIDTH), bf16),
        ),
        in_specs=[any_spec] * 3 + [vmem] * 4,
        out_specs=[any_spec] * 3,
        scratch_shapes=[
            V(SLAB, WIDTH),
            V(SLAB, WIDTH),
            V(24, BLK, dtype=f32),
            V(STEPS, EXT, BLK),
            V(STEPS, OWN, BLK),
            V(EXT // BLK * 8, BLK, dtype=f32),
            V(24, BLK, dtype=f32),
            V(EXT, BLK, dtype=f32),
            V(STEPS, 2, BLK, NY * BLK),
            V(STEPS, 2, BLK, NY * BLK),
            V(STEPS, 2, BLK, NY * BLK),
            V(STEPS, 3, 2, BLK, NY * BLK),
            V(STEPS, 2, BLK, NY * BLK),
            V(STEPS, NY, 2, BLK, BLK),
            V(STEPS, 2, TXT, BLK),
            V(KEYS, 2 * BLK),
            V(BLK, KEYS),
            V(BLK + 16, KEYS),
            V(QT, 2 * BLK),
            V(QT, 2 * BLK),
            V(NCHUNK, KC, QT, dtype=f32),
            V(NCHUNK, KC, QT),
            V(NCHUNK, KC, QT),
            V(BLK, QT),
            V(BLK, QT),
            V(8, QT, dtype=f32),
            V(8, QT, dtype=f32),
            V(KEYS, BLK, dtype=f32),
            V(KEYS, BLK, dtype=f32),
            V(OWN, BLK, dtype=f32),
            V(STEPS, OWN, BLK),
            V(2, OWN, BLK, dtype=f32),
            V(STEPS, 2, SLAB, BLK),
            V(STEPS, 2, SLAB, BLK),
            V(STEPS, OWN, BLK),
            V(SLAB, WIDTH),
            V(OWN, BLK, dtype=f32),
            V(2, SLAB, BLK, dtype=f32),
            V(96, BLK, dtype=f32),
            V(2, 24, BLK, dtype=f32),
            V(2, 24, BLK, dtype=f32),
            V(NY, 24, BLK, dtype=f32),
            V(STEPS, 2, TXT, BLK),
            V(STEPS, NX, 2, BLK, BLK),
            V(STEPS, 2, BLK, BLK),
            V(STEPS, BLK, NY * BLK),
            V(STEPS, TXT, BLK),
            V(SLAB, WIDTH),
            pltpu.SemaphoreType.DMA((KINDS, STEPS, 8)),
            pltpu.SemaphoreType.DMA((KINDS, STEPS, 8)),
            pltpu.SemaphoreType.DMA((5, 4)),
            pltpu.SemaphoreType.DMA((5, 4)),
            pltpu.SemaphoreType.DMA((8, STEPS)),
            pltpu.SemaphoreType.DMA((2,)),
        ],
        compiler_params=pltpu.CompilerParams(
            collective_id=0, has_side_effects=True, vmem_limit_bytes=60 * 1024 * 1024
        ),
        cost_estimate=pl.CostEstimate(
            flops=24 * 10**9, bytes_accessed=40 * 10**6, transcendentals=12 * 10**6
        ),
        name="attention",
    )(
        hidden[0],
        grad_out[0],
        text_kv[0, 0],
        query_norm_gain,
        key_norm_gain,
        select,
        qbias,
    )
    return (attended[None], upstream[None], text_total[None])


def solution(mesh):
    in_specs = (
        P("section", "seq", None),
        P("section", None),
        P("section", None),
        P("section", "seq", None, None, None),
        P("section"),
        P(),
        P("section", "seq", None),
    )
    out_specs = (
        P("section", "seq", None),
        P("section", "seq", None),
        P("section", None, None, None),
    )
    return jax.shard_map(local, mesh=mesh, in_specs=in_specs, out_specs=out_specs, check_vma=False)
```
